512 devices in a mesh: ctx: 32 (over x_lo, z), head: 16 (over x_hi, y, core).
Axes of the slice: x: 4 (x_hi: 2, x_lo: 2; x = x_hi * 2 + x_lo), y: 4, z: 16, core: 2. Of those that a mesh axis runs over, the one named last changes fastest.
Arguments:
- q_latent: bfloat16 [4096, 1536], P('ctx'), may hold values from -6 to 6
- latent_bias: float32 [32, 1536], P('ctx'), may hold values from -3 to 3
- norm_gain: float32 [1536], replicated, may hold values from 0.5 to 1.5
- w_q: bfloat16 [1536, 24576], P('ctx', 'head'), may hold values from -0.15625 to 0.15625
- steer: float32 [32, 24576], P('ctx', 'head'), may hold values from -10 to 10
- kv_latent: bfloat16 [4096, 512], P('ctx'), may hold values from -6 to 6
- key_rope: bfloat16 [4096, 64], P('ctx'), may hold values from -10 to 10
- w_uk: bfloat16 [512, 16384], P(None, 'head'), may hold values from -0.25 to 0.25
- w_uv: bfloat16 [512, 16384], P(None, 'head'), may hold values from -0.25 to 0.25
- d_out: bfloat16 [4096, 16384], P('ctx', 'head'), may hold values from -0.29882812 to 0.29882812
- block_mask: int32 [32, 32], replicated, may hold values from 0 to 1, as said below
Outputs:
- grad_steer: float32 [32, 24576], P('ctx', 'head')
- grad_latent_bias: float32 [32, 1536], P('ctx')
The draws below stay inside these ranges and needn't reach their ends.
Inputs may be any that keep to these rules, and one draw needn't show every extreme that they name: `block_mask`: query block i always attends key block i; its other entries are 1 at a rate drawn per query block among 1/16, 2/16, 4/16 and 7/16.
All inputs are finite; a program needn't handle non-finite values.
Results may differ from the reference program's by a relative error of at most 0.024.
Values may be sent and summed in bfloat16 or wider, within the bound.
A program may use at most 64 MiB of HBM per device.

```python
import jax
import jax.numpy as jnp
from jax import lax

H = 128
QL = 1536
KVL = 512
NOPE = 128
ROPE = 64
VD = 128
BLK = 128
QUERIES = 4096
KEYS = 4096
QB = 32
KB = 32


def draw_block_mask(key, part):
    first_key, second_key = jax.random.split(key)
    level = jax.random.randint(first_key, (QB, 1), 0, 4)
    rate = 1 + level * (level + 1) // 2
    rolls = jax.random.randint(second_key, (QB, KB), 0, 16)
    own_col = (jnp.arange(QB, dtype=jnp.int32) * KB // QB)[:, None]
    columns = jnp.arange(KB, dtype=jnp.int32)[None, :]
    return jnp.where((rolls < rate) | (columns == own_col), 1, 0).astype(jnp.int32)


def draw_steer(key, part):
    first_key = jax.random.fold_in(key, 0)
    head_width = NOPE + ROPE
    values = jnp.clip(0.5 * jax.random.normal(first_key, (QB, H, head_width), jnp.float32), -2.5, 2.5)
    return values.reshape(QB, H * head_width).astype(jnp.float32)


def draw_key_rope(key, part):
    first_key = jax.random.fold_in(key, 0)
    values = jnp.clip(jax.random.normal(first_key, (KEYS, ROPE), jnp.float32), -4.0, 4.0)
    return values.astype(jnp.bfloat16)


def shard_levels(own_key, dims, pieces, least, high):
    factor_of = 1.0
    for position, parts in pieces:
        draws = jax.random.uniform(jax.random.fold_in(jax.random.fold_in(own_key, 6), position), (parts,), jnp.float32, least / len(pieces), high / len(pieces))
        factor_of = factor_of * jnp.repeat(jnp.exp(draws), dims[position] // parts).reshape((-1,) + (1,) * (len(dims) - 1 - position))
    return factor_of


def scatter_about(rng, dims, scale, limit, pieces=(), kind=jnp.bfloat16):
    entries = scale * jax.random.normal(rng, dims, jnp.float32)
    if pieces:
        entries = entries * shard_levels(rng, dims, pieces, -0.22, 0.18)
    return jnp.clip(entries, -limit, limit).astype(kind)


def setup_inputs(seed: int = 0) -> dict:
    splits = jax.random.split(jax.random.key(seed), 12)
    q_latent = scatter_about(splits[0], (QUERIES, QL), 1.0, 6.0, ((0, 32),))
    latent_bias = scatter_about(splits[1], (QB, QL), 0.5, 3.0, ((0, 32),), jnp.float32)
    norm_gain = jnp.clip(1.0 + 0.1 * jax.random.normal(splits[2], (QL,), jnp.float32), 0.5, 1.5)
    w_q = scatter_about(splits[3], (QL, H * (NOPE + ROPE)), QL ** -0.5, 0.15625, ((0, 32), (1, 16)))
    steer = draw_steer(jax.random.fold_in(splits[11], 71), 0)
    kv_latent = scatter_about(splits[5], (KEYS, KVL), 1.0, 6.0, ((0, 32),))
    key_rope = draw_key_rope(jax.random.fold_in(splits[11], 71), 0)
    w_uk = scatter_about(splits[7], (KVL, H * NOPE), KVL ** -0.5, 0.25, ((1, 16),))
    w_uv = scatter_about(splits[8], (KVL, H * VD), KVL ** -0.5, 0.25, ((1, 16),))
    d_out = scatter_about(splits[9], (QUERIES, H * VD), 0.05, 0.29882812, ((0, 32), (1, 16)))
    block_mask = draw_block_mask(jax.random.fold_in(splits[11], 71), 0)
    return {"q_latent": q_latent, "latent_bias": latent_bias, "norm_gain": norm_gain, "w_q": w_q, "steer": steer, "kv_latent": kv_latent, "key_rope": key_rope, "w_uk": w_uk, "w_uv": w_uv, "d_out": d_out, "block_mask": block_mask}


epsilon = 1e-06

def rounded(values):
    return lax.optimization_barrier(values.astype(jnp.bfloat16)).astype(jnp.float32)

def reference(q_latent, latent_bias, norm_gain, w_q, steer, kv_latent, key_rope, w_uk, w_uv, d_out, block_mask):
    head_width = NOPE + ROPE
    score_scale = head_width ** (-0.5)
    row_count = BLK * H
    highest = lax.Precision.HIGHEST
    lat_blocks = kv_latent.astype(jnp.float32).reshape(KB, BLK, KVL)
    rope_blocks = key_rope.astype(jnp.float32).reshape(KB, BLK, ROPE)
    wq_full = w_q.astype(jnp.float32)
    key_up = w_uk.astype(jnp.float32).reshape(KVL, H, NOPE)
    value_up = w_uv.astype(jnp.float32).reshape(KVL, H, VD)

    def one_block(index):
        latent_rows = lax.dynamic_slice_in_dim(q_latent, index * BLK, BLK, 0).astype(jnp.float32)
        shifted = latent_rows + lax.dynamic_slice_in_dim(latent_bias, index, 1, 0)
        inv_rms = lax.rsqrt(lax.optimization_barrier(jnp.mean(shifted * shifted, axis=1, keepdims=True)) + epsilon)
        normed = shifted * inv_rms
        c_query = rounded(normed * norm_gain)
        projected = jnp.dot(c_query, wq_full, precision=highest, preferred_element_type=jnp.float32)
        query_all = rounded(projected + lax.dynamic_slice_in_dim(steer, index, 1, 0)).reshape(BLK, H, head_width)
        q_absorbed = rounded(jnp.einsum('qhn,khn->qhk', query_all[:, :, :NOPE], key_up, precision=highest)).reshape(row_count, KVL)
        q_rope = query_all[:, :, NOPE:].reshape(row_count, ROPE)
        grad_out = lax.dynamic_slice_in_dim(d_out, index * BLK, BLK, 0).astype(jnp.float32).reshape(BLK, H, VD)
        g_absorbed = rounded(jnp.einsum('qhv,khv->qhk', grad_out, value_up, precision=highest)).reshape(row_count, KVL)
        mask_row = lax.dynamic_index_in_dim(block_mask, index, 0, keepdims=False)

        def visit_block(status, inputs):
            lat_tile, rope_tile, flag = inputs

            def update(status):
                peak, total_weight, weighted, lat_acc, rope_acc = status
                scores = (jnp.dot(q_absorbed, lat_tile.T, precision=highest) + jnp.dot(q_rope, rope_tile.T, precision=highest)) * score_scale
                new_peak = jnp.maximum(peak, lax.optimization_barrier(jnp.max(scores, axis=1)))
                factor = jnp.exp(peak - new_peak)
                weights = jnp.exp(scores - new_peak[:, None])
                dots = jnp.dot(g_absorbed, lat_tile.T, precision=highest)
                mixed = weights * dots
                total_weight = total_weight * factor + lax.optimization_barrier(jnp.sum(weights, axis=1))
                weighted = weighted * factor + lax.optimization_barrier(jnp.sum(mixed, axis=1))
                stacked = rounded(jnp.concatenate([mixed, weights], axis=0))
                doubled = jnp.concatenate([factor, factor])[:, None]
                lat_acc = lat_acc * doubled + jnp.dot(stacked, lat_tile, precision=highest)
                rope_acc = rope_acc * doubled + jnp.dot(stacked, rope_tile, precision=highest)
                return (new_peak, total_weight, weighted, lat_acc, rope_acc)

            def keep_status(status):
                return status
            return (lax.cond(flag > 0, update, keep_status, status), None)
        start_status = (jnp.full((row_count,), -1e+30, jnp.float32), jnp.zeros((row_count,), jnp.float32), jnp.zeros((row_count,), jnp.float32), jnp.zeros((2 * row_count, KVL), jnp.float32), jnp.zeros((2 * row_count, ROPE), jnp.float32))
        final, unused = lax.scan(visit_block, start_status, (lat_blocks, rope_blocks, mask_row))
        peak, total_weight, weighted, lat_acc, rope_acc = final
        ratio = (weighted / total_weight)[:, None]
        inverse = (score_scale / total_weight)[:, None]
        grad_lat = rounded((lat_acc[:row_count] - ratio * lat_acc[row_count:]) * inverse)
        grad_rope = (rope_acc[:row_count] - ratio * rope_acc[row_count:]) * inverse
        grad_nope = jnp.einsum('qhk,khn->qhn', grad_lat.reshape(BLK, H, KVL), key_up, precision=highest)
        grad_query = jnp.concatenate([grad_nope, grad_rope.reshape(BLK, H, ROPE)], axis=2).reshape(BLK, H * head_width)
        steer_grad = lax.optimization_barrier(jnp.sum(grad_query, axis=0))
        latent_grad = jnp.dot(rounded(grad_query), wq_full.T, precision=highest)
        scaled = latent_grad * norm_gain
        project_mean = lax.optimization_barrier(jnp.mean(scaled * normed, axis=1, keepdims=True))
        grad_shifted = inv_rms * (scaled - normed * project_mean)
        return (steer_grad, lax.optimization_barrier(jnp.sum(grad_shifted, axis=0)))
    grad_steer, grad_latent_bias = lax.map(one_block, jnp.arange(QB, dtype=jnp.int32))
    return (grad_steer, grad_latent_bias)
```

```python
import functools
import math

import jax
import jax.numpy as jnp
from jax import lax
from jax.experimental import pallas as pl
from jax.experimental.pallas import tpu as pltpu
from jax.sharding import PartitionSpec as P

KVL = 512
NOPE = 128
ROPE = 64
BLK = 128
WIDE = 640
HALF = 4
HEADW = NOPE + ROPE
QCOLS = HALF * HEADW
QTWO = QCOLS // 2
DCOLS = HALF * NOPE
EPS = 1e-06
LOWEST = -1e30
NZ = 16
NY = 4
MESH = pl.DeviceIdType.MESH
F32 = jnp.float32
BF16 = jnp.bfloat16
ANY = pl.BlockSpec(memory_space=pl.ANY)
HBM = pl.BlockSpec(memory_space=pltpu.HBM)
VM = pl.BlockSpec(memory_space=pltpu.VMEM)


def last_last(left, right):
    return lax.dot_general(left, right, (((1,), (1,)), ((), ())), preferred_element_type=F32)


def place():
    c = lax.axis_index("ctx")
    k = lax.axis_index("head")
    return c, k, c // NZ, lax.rem(c, NZ)


def gather_kernel(
    w_ref, q_ref, b_ref, s_ref, d_ref, kv_ref, kr_ref,
    W, KV, Xq, Xb, Xs, Xd,
    own, rope,
    w_s, w_r, z_s, z_r, y_s, y_r, f_s, f_r, x_s, x_r, c_s, c_r, m_s, m_r, loc,
):
    c, k, a, z = place()
    x_hi = k // 8
    y = lax.rem(k, 8) // 2
    core = lax.rem(k, 2)
    z_right = (a * NZ + lax.rem(z + 1, NZ), k)
    z_left = (a * NZ + lax.rem(z + NZ - 1, NZ), k)
    z_right2 = (a * NZ + lax.rem(z + 2, NZ), k)
    z_left2 = (a * NZ + lax.rem(z + NZ - 2, NZ), k)
    y_right = (c, x_hi * 8 + lax.rem(y + 1, NY) * 2 + core)
    y_left = (c, x_hi * 8 + lax.rem(y + NY - 1, NY) * 2 + core)
    sibling = (c, x_hi * 8 + y * 2 + (1 - core))
    pair = ((1 - a) * NZ + z, k)
    across = ((1 - a) * NZ + z, (1 - x_hi) * 8 + y * 2 + core)

    barrier = pltpu.get_barrier_semaphore()
    for dev in (z_right, z_left, z_right2, z_left2, y_right, y_left, sibling, pair, across):
        pl.semaphore_signal(barrier, inc=1, device_id=dev, device_id_type=MESH)

    load_k = pltpu.make_async_copy(kv_ref, own.at[:, pl.ds(0, KVL)], loc.at[2])
    load_r = pltpu.make_async_copy(kr_ref, rope, loc.at[3])
    load_k.start()
    load_r.start()
    load_r.wait()
    own[:, KVL:] = jnp.concatenate([rope[...], jnp.zeros((BLK, WIDE - KVL - ROPE), BF16)], axis=1)
    load_k.wait()
    pl.semaphore_wait(barrier, 9)

    sends = []

    def send(src, dst, s, r, dev):
        copy = pltpu.make_async_remote_copy(
            src_ref=src, dst_ref=dst, send_sem=s, recv_sem=r, device_id=dev, device_id_type=MESH
        )
        copy.start()
        sends.append(copy)

    def got(dst, s, r):
        pltpu.make_async_remote_copy(
            src_ref=dst, dst_ref=dst, send_sem=s, recv_sem=r, device_id=pair, device_id_type=MESH
        ).wait_recv()

    def columns(who, two):
        return pl.ds(pl.multiple_of(who * QCOLS + two * QTWO, 128), QTWO)

    their_d = pl.ds(pl.multiple_of((1 - a) * DCOLS, 128), DCOLS)

    counts = {(0, 0): 8, (0, 1): 7, (1, 0): 7, (1, 1): 8}

    def w_slot(part, two, zz):
        return W.at[two, (a if part == 0 else 1 - a) * NZ + lax.rem(zz + 2 * NZ, NZ)]

    def w_send(way, part, two, step):
        at = z - (step - 1) if way == 0 else z + (step - 1)
        slot = w_slot(part, two, at)
        src = w_ref.at[:, columns(a, two)] if step == 1 and part == 0 else slot
        n = 4 * way + 2 * part + two
        send(src, slot, w_s.at[n, step - 1], w_r.at[n, step - 1], z_left if way else z_right)

    def w(step):
        for part, two in ((0, 0), (0, 1), (1, 0), (1, 1)):
            for way in (0, 1):
                if step <= counts[way, part]:
                    n = 4 * way + 2 * part + two
                    at = z + step if way else z - step
                    got(w_slot(part, two, at), w_s.at[n, step - 1], w_r.at[n, step - 1])
                    if step + 1 <= counts[way, part]:
                        w_send(way, part, two, step + 1)

    rows = pl.ds(pl.multiple_of(core * 64 + y * 16, 16), 16)

    def far(way, step):
        return 0 if step == 0 else (2 * step if way else 2 * step - 1)

    def z_send(way, step):
        hop = 1 if step == 1 else 2
        src = own.at[rows] if step <= 2 else KV.at[a, far(way, step - 2), rows]
        dev = (z_left if way else z_right) if hop == 1 else (z_left2 if way else z_right2)
        send(src, KV.at[a, far(way, step), rows], z_s.at[way, step - 1], z_r.at[way, step - 1], dev)

    def kz(step):
        for way in range(2):
            if step <= 8 - way:
                got(KV.at[a, far(way, step), rows], z_s.at[way, step - 1], z_r.at[way, step - 1])
                if step + 2 <= 8 - way:
                    z_send(way, step + 2)

    def y_rows(shift):
        return pl.ds(pl.multiple_of(core * 64 + lax.rem(y + shift + NY, NY) * 16, 16), 16)

    def ky(q):
        part = KV.at[a, pl.ds(4 * q, 4), rows]
        send(part, part, y_s.at[0, q], y_r.at[0, q], y_right)
        send(part, part, y_s.at[1, q], y_r.at[1, q], y_left)

    def kf(q):
        for way in range(2):
            shift = 1 if way else -1
            got(KV.at[a, pl.ds(4 * q, 4), y_rows(shift)], y_s.at[way, q], y_r.at[way, q])
            part = KV.at[a, pl.ds(4 * q + 2 * way, 2), y_rows(shift)]
            send(part, part, f_s.at[way, q], f_r.at[way, q], y_left if way else y_right)

    half = pl.ds(pl.multiple_of(core * 64, 16), 64)

    def split(q):
        near = 16 if q < 2 else 32
        return (
            pl.ds(pl.multiple_of(core * 64, 16), near),
            pl.ds(pl.multiple_of(core * 64 + near, 16), 64 - near),
        )

    def kx(q):
        for way in range(2):
            got(KV.at[a, pl.ds(4 * q + 2 * way, 2), y_rows(2)], f_s.at[way, q], f_r.at[way, q])
        near_rows, far_rows = split(q)
        part = KV.at[a, pl.ds(4 * q, 4), far_rows]
        send(part, part, x_s.at[1, q], x_r.at[1, q], across)
        part = KV.at[a, pl.ds(4 * q, 4), near_rows]
        send(part, part, x_s.at[0, q], x_r.at[0, q], pair)
        part = KV.at[a, pl.ds(4 * q, 4), half]
        send(part, part, c_s.at[0, q], c_r.at[0, q], sibling)

    def kc(q):
        near_rows, far_rows = split(q)
        got(KV.at[1 - a, pl.ds(4 * q, 4), near_rows], x_s.at[0, q], x_r.at[0, q])
        got(KV.at[1 - a, pl.ds(4 * q, 4), far_rows], x_s.at[1, q], x_r.at[1, q])
        part = KV.at[1 - a, pl.ds(4 * q, 4), half]
        send(part, part, c_s.at[1, q], c_r.at[1, q], sibling)

    for two in range(2):
        send(w_ref.at[:, columns(1 - a, two)], W.at[two, c], m_s.at[6 * two], m_r.at[6 * two], pair)
    for step in (1, 2):
        z_send(0, step)
        z_send(1, step)
    for two in range(2):
        w_send(0, 0, two, 1)
        w_send(1, 0, two, 1)
    copy_w = [pltpu.make_async_copy(w_ref.at[:, columns(a, two)], W.at[two, c], loc.at[4 * two]) for two in range(2)]
    for copy in copy_w:
        copy.start()
    copy_k = pltpu.make_async_copy(own.at[rows], KV.at[a, 0, rows], loc.at[1])
    copy_k.start()
    q_rows = pl.ds(pl.multiple_of(core * 64, 16), 64)
    send(q_ref.at[q_rows], Xq.at[q_rows], m_s.at[1], m_r.at[1], pair)
    send(d_ref.at[:, their_d], Xd, m_s.at[3], m_r.at[3], pair)
    send(b_ref, Xb, m_s.at[4], m_r.at[4], pair)
    send(s_ref, Xs, m_s.at[5], m_r.at[5], pair)
    for two in range(2):
        got(w_slot(1, two, z), m_s.at[6 * two], m_r.at[6 * two])
        w_send(0, 1, two, 1)
        w_send(1, 1, two, 1)

    kz(1)
    w(1)
    kz(2)
    copy_k.wait()
    ky(0)
    w(2)
    kz(3)
    kf(0)
    kz(4)
    ky(1)
    w(3)
    kx(0)
    kz(5)
    kf(1)
    kz(6)
    ky(2)
    w(4)
    kx(1)
    kc(0)
    kz(7)
    kf(2)
    kz(8)
    ky(3)
    w(5)
    kc(1)
    got(Xq.at[q_rows], m_s.at[1], m_r.at[1])
    send(Xq.at[q_rows], Xq.at[q_rows], m_s.at[2], m_r.at[2], sibling)
    kx(2)
    w(6)
    kf(3)
    kc(2)
    w(7)
    kx(3)
    w(8)
    kc(3)

    other = pl.ds(pl.multiple_of((1 - core) * 64, 16), 64)
    for q in range(4):
        got(KV.at[a, pl.ds(4 * q, 4), other], c_s.at[0, q], c_r.at[0, q])
        got(KV.at[1 - a, pl.ds(4 * q, 4), other], c_s.at[1, q], c_r.at[1, q])
    got(Xq.at[other], m_s.at[2], m_r.at[2])
    got(Xd, m_s.at[3], m_r.at[3])
    got(Xb, m_s.at[4], m_r.at[4])
    got(Xs, m_s.at[5], m_r.at[5])
    for copy in copy_w:
        copy.wait()
    for copy in sends:
        copy.wait_send()


def gather(w_q, q_latent, latent_bias, steer, d_out, kv_latent, key_rope):
    def dma(*shape):
        return pltpu.SemaphoreType.DMA(shape)

    return pl.pallas_call(
        gather_kernel,
        out_shape=(
            jax.ShapeDtypeStruct((2, 2 * NZ, w_q.shape[0], QTWO), BF16),
            jax.ShapeDtypeStruct((2, NZ, BLK, WIDE), BF16),
            jax.ShapeDtypeStruct(q_latent.shape, BF16),
            jax.ShapeDtypeStruct(latent_bias.shape, F32),
            jax.ShapeDtypeStruct(steer.shape, F32),
            jax.ShapeDtypeStruct((BLK, DCOLS), BF16),
        ),
        in_specs=[HBM] * 7,
        out_specs=[ANY] * 6,
        scratch_shapes=[
            pltpu.VMEM((BLK, WIDE), BF16),
            pltpu.VMEM((BLK, ROPE), BF16),
            dma(8, 8), dma(8, 8), dma(2, 8), dma(2, 8), dma(2, 4), dma(2, 4), dma(2, 4), dma(2, 4),
            dma(2, 4), dma(2, 4), dma(2, 4), dma(2, 4), dma(7), dma(7), dma(5),
        ],
        compiler_params=pltpu.CompilerParams(
            collective_id=0, has_side_effects=True, vmem_limit_bytes=54 * 2**20
        ),
        cost_estimate=pl.CostEstimate(flops=0, bytes_accessed=20_000_000, transcendentals=0),
        name="gather",
    )(w_q, q_latent, latent_bias, steer, d_out, kv_latent, key_rope)


CHUNK = 256
TILES = CHUNK // BLK


def attend_kernel(
    mask, q_ref, xq_ref, b_ref, xb_ref, gain_ref, W_ref, s_ref, xs_ref, KV, uk_ref, uv_ref, d_ref, xd_ref,
    gs_ref, lb_ref,
    Wv, q2, uk, uv, dv, kvc, cq, pj, qg, qr, sbuf, dbuf, acc, gl, gr, peak, lsum, gsum, u_ref,
    sem, kv_sem,
):
    c, k, a, z = place()
    gain = gain_ref[...].reshape(1, gain_ref.shape[0])
    scale = HEADW ** (-0.5)
    scale2 = scale * math.log2(math.e)
    rows = HALF * BLK
    my_d = pl.ds(pl.multiple_of(a * DCOLS, 128), DCOLS)
    loads = [
        pltpu.make_async_copy(q_ref, q2.at[0], sem.at[0]),
        pltpu.make_async_copy(W_ref, Wv, sem.at[1]),
        pltpu.make_async_copy(uk_ref.at[:, my_d], uk, sem.at[2]),
        pltpu.make_async_copy(uv_ref.at[:, my_d], uv, sem.at[3]),
        pltpu.make_async_copy(d_ref.at[:, my_d], dv.at[0], sem.at[4]),
        pltpu.make_async_copy(xq_ref, q2.at[1], sem.at[5]),
        pltpu.make_async_copy(xd_ref, dv.at[1], sem.at[6]),
    ]
    for copy in loads:
        copy.start()

    def tile_copy(i, j, n):
        far = lax.rem(z - lax.rem(j, NZ) + NZ, NZ)
        slot = jnp.where(far == 0, 0, jnp.where(far <= NZ // 2, 2 * far - 1, 2 * (NZ - far)))
        return pltpu.make_async_copy(KV.at[j // NZ, slot], kvc.at[i, n], kv_sem.at[i, n])

    live = []
    for i in range(2):
        block = c if i == 0 else lax.rem(c + NZ, 2 * NZ)

        def visit(j, n):
            on = mask[block, j] > 0

            @pl.when(on)
            def _():
                tile_copy(i, j, n).start()

            return n + jnp.where(on, 1, 0)

        live.append(lax.fori_loop(0, 2 * NZ, visit, 0))

    def chunks_of(n):
        return (n + TILES - 1) // TILES

    for i in range(2):
        n = live[i]
        for extra in range(TILES - 1):
            @pl.when(n + extra < chunks_of(n) * TILES)
            def _():
                kvc[i, n + extra] = jnp.zeros((BLK, WIDE), BF16)

    def keys_of(i, t):
        return kvc[i, pl.ds(t * TILES, TILES)].reshape(CHUNK, WIDE)

    invs = []
    for i in range(2):
        loads[5 * i].wait()
        shifted = q2[i].astype(F32) + (b_ref, xb_ref)[i][...]
        invs.append(lax.rsqrt(jnp.mean(shifted * shifted, axis=1, keepdims=True) + EPS))
        cq[i] = (shifted * invs[i] * gain).astype(BF16)
    both = 2 * BLK
    loads[3].wait()
    loads[4].wait()
    loads[6].wait()
    for h in range(HALF):
        up = slice(h * NOPE, (h + 1) * NOPE)
        g = last_last(dv[:, :, up].reshape(both, NOPE), uv[:, up]).astype(BF16)
        for i in range(2):
            qg[i, rows + h * BLK : rows + (h + 1) * BLK, :] = g[i * BLK : (i + 1) * BLK]
    loads[1].wait()
    loads[2].wait()
    c_query = cq[...].reshape(both, cq.shape[2])
    for two in range(2):
        proj = jnp.dot(c_query, Wv[two], preferred_element_type=F32)
        pj[:, two * QTWO : (two + 1) * QTWO] = proj
        for i in range(2):
            row = (s_ref, xs_ref)[i]
            part = slice(two * QTWO, (two + 1) * QTWO)
            other = slice(QCOLS + two * QTWO, QCOLS + (two + 1) * QTWO)
            cq[i, :, part] = (proj[i * BLK : (i + 1) * BLK] + jnp.where(a == 0, row[:, part], row[:, other])).astype(BF16)
    query = cq[:, :, :QCOLS].reshape(both, QCOLS)
    for h in range(HALF):
        at = h * HEADW
        q = last_last(query[:, at : at + NOPE], uk[:, h * NOPE : (h + 1) * NOPE]).astype(BF16)
        rope = query[:, at + NOPE : at + HEADW]
        rope = jnp.concatenate([rope, jnp.zeros((both, WIDE - KVL - ROPE), BF16)], axis=1)
        for i in range(2):
            qg[i, h * BLK : (h + 1) * BLK, :] = q[i * BLK : (i + 1) * BLK]
            qr[i, h * BLK : (h + 1) * BLK, :] = rope[i * BLK : (i + 1) * BLK]

    def in_pairs(count, step):
        def pair(t, _):
            step(2 * t, 2)
            return 0

        lax.fori_loop(0, count // 2, pair, 0)

        @pl.when(lax.rem(count, 2) == 1)
        def _():
            step(count - 1, 1)

    for i in range(2):
        n = live[i]
        count = chunks_of(n)

        def arrived(t, _):
            tile_copy(i, 0, t).wait()
            return 0

        lax.fori_loop(0, n, arrived, 0)
        peak[...] = jnp.full((rows, 128), LOWEST, F32)
        lsum[...] = jnp.zeros((rows, 128), F32)
        gsum[...] = jnp.zeros((rows, 128), F32)
        acc[...] = jnp.zeros((rows, WIDE), F32)

        def scores(first, many):
            top = peak[...]
            for t in [first + d for d in range(many)]:
                keys = keys_of(i, t)
                column = lax.broadcasted_iota(jnp.int32, (1, CHUNK), 1) + t * CHUNK
                dead = jnp.where(column < n * BLK, 0.0, LOWEST)
                main = last_last(qg[i], keys[:, :KVL])
                s = main[:rows] + last_last(qr[i], keys[:, KVL:]) + dead
                sbuf[t] = s
                dbuf[t] = main[rows:]
                for part in range(TILES):
                    top = jnp.maximum(top, s[:, part * 128 : (part + 1) * 128])
            peak[...] = top

        in_pairs(count, scores)
        top = jnp.max(peak[...], axis=1, keepdims=True) * scale2

        def weigh(first, many):
            low = lsum[...]
            gow = gsum[...]
            for t in [first + d for d in range(many)]:
                e = jnp.exp2(sbuf[t] * scale2 - top)
                sbuf[t] = e
                mixed = e * dbuf[t]
                low = low + sum(e[:, p * 128 : (p + 1) * 128] for p in range(TILES))
                gow = gow + sum(mixed[:, p * 128 : (p + 1) * 128] for p in range(TILES))
            lsum[...] = low
            gsum[...] = gow

        in_pairs(count, weigh)
        total = jnp.sum(lsum[...], axis=1, keepdims=True)
        ratio = jnp.sum(gsum[...], axis=1, keepdims=True) / total

        def collect(first, many):
            weight = jnp.concatenate(
                [(sbuf[first + d] * (dbuf[first + d] - ratio)).astype(BF16) for d in range(many)], axis=1
            )
            keys = kvc[i, pl.ds(first * TILES, many * TILES)].reshape(many * CHUNK, WIDE)
            acc[...] += jnp.dot(weight, keys, preferred_element_type=F32)

        in_pairs(count, collect)
        grad = acc[...] * (scale / total)
        gl[i] = grad[:, :KVL].astype(BF16).reshape(HALF, BLK, KVL)
        gr[i] = grad[:, KVL:].reshape(HALF, BLK, WIDE - KVL)

    pieces = []
    for h in range(HALF):
        pieces.append(
            jnp.dot(gl[:, h].reshape(both, KVL), uk[:, h * NOPE : (h + 1) * NOPE], preferred_element_type=F32)
        )
        pieces.append(gr[:, h].reshape(both, WIDE - KVL)[:, :ROPE])
    all_grads = jnp.concatenate(pieces, axis=1)
    for i in range(2):
        grad_query = all_grads[i * BLK : (i + 1) * BLK]
        gs_ref[i : i + 1, :] = jnp.sum(grad_query, axis=0, keepdims=True)
        lean = jnp.sum(grad_query * pj[i * BLK : (i + 1) * BLK, :], axis=1, keepdims=True)
        u = jnp.sum(grad_query * invs[i], axis=0, keepdims=True)
        u_high = u.astype(BF16)
        u_ref[2 * i : 2 * i + 1, :] = u_high.astype(F32)
        u_ref[2 * i + 1 : 2 * i + 2, :] = u - u_high.astype(F32)
        shifted = q2[i].astype(F32) + (b_ref, xb_ref)[i][...]
        lb_ref[i : i + 1, :] = jnp.sum(shifted * (invs[i] * invs[i] * lean), axis=0, keepdims=True)

    back = sum(
        last_last(u_ref[:, two * QTWO : (two + 1) * QTWO].astype(BF16), Wv[two]) for two in range(2)
    )
    for i in range(2):
        whole = back[2 * i : 2 * i + 1] + back[2 * i + 1 : 2 * i + 2]
        lb_ref[i : i + 1, :] = gain * whole - lb_ref[i : i + 1, :] * (1.0 / gain.shape[1])


def attend(mask, q, xq, b, xb, gain, W, s, xs, KV, w_uk, w_uv, d, xd):
    ql = q.shape[1]
    rows = HALF * BLK
    nchunk = 2 * NZ // TILES
    return pl.pallas_call(
        attend_kernel,
        out_shape=(jax.ShapeDtypeStruct((2, QCOLS), F32), jax.ShapeDtypeStruct((2, ql), F32)),
        in_specs=[
            pl.BlockSpec(memory_space=pltpu.SMEM), HBM, ANY, VM, VM, VM, ANY, VM, VM, ANY, HBM, HBM, HBM, ANY,
        ],
        out_specs=[VM, VM],
        scratch_shapes=[
            pltpu.VMEM((2, ql, QTWO), BF16),
            pltpu.VMEM((2, BLK, ql), BF16),
            pltpu.VMEM((KVL, DCOLS), BF16),
            pltpu.VMEM((KVL, DCOLS), BF16),
            pltpu.VMEM((2, BLK, DCOLS), BF16),
            pltpu.VMEM((2, 2 * NZ, BLK, WIDE), BF16),
            pltpu.VMEM((2, BLK, ql), BF16),
            pltpu.VMEM((2 * BLK, QCOLS), F32),
            pltpu.VMEM((2, 2 * rows, KVL), BF16),
            pltpu.VMEM((2, rows, WIDE - KVL), BF16),
            pltpu.VMEM((nchunk, rows, CHUNK), F32),
            pltpu.VMEM((nchunk, rows, CHUNK), F32),
            pltpu.VMEM((rows, WIDE), F32),
            pltpu.VMEM((2, HALF, BLK, KVL), BF16),
            pltpu.VMEM((2, HALF, BLK, WIDE - KVL), F32),
            pltpu.VMEM((rows, 128), F32),
            pltpu.VMEM((rows, 128), F32),
            pltpu.VMEM((rows, 128), F32),
            pltpu.VMEM((16, QCOLS), F32),
            pltpu.SemaphoreType.DMA((7,)),
            pltpu.SemaphoreType.DMA((2, 2 * NZ)),
        ],
        compiler_params=pltpu.CompilerParams(vmem_limit_bytes=54 * 2**20),
        cost_estimate=pl.CostEstimate(flops=10_000_000_000, bytes_accessed=10_000_000, transcendentals=4_000_000),
        name="attend",
    )(mask, q, xq, b, xb, gain, W, s, xs, KV, w_uk, w_uv, d, xd)


def reduce_kernel(gs_ref, lb_ref, steer_out, bias_out, total, rbuf, rgs, rlb, p_s, p_r, g_s, g_r):
    c, k, a, z = place()
    pair = ((1 - a) * NZ + z, k)
    n = 16

    def mate(shift):
        return (c, lax.rem(k + shift + n, n))

    barrier = pltpu.get_barrier_semaphore()
    pl.semaphore_signal(barrier, inc=1, device_id=pair, device_id_type=MESH)
    for shift in range(1, n):
        pl.semaphore_signal(barrier, inc=1, device_id=mate(shift), device_id_type=MESH)
    pl.semaphore_wait(barrier, n)

    def copy(src, dst, s, r, dev):
        return pltpu.make_async_remote_copy(
            src_ref=src, dst_ref=dst, send_sem=s, recv_sem=r, device_id=dev, device_id_type=MESH
        )

    first = copy(lb_ref.at[pl.ds(1, 1)], rlb, p_s.at[0], p_r.at[0], pair)
    second = copy(gs_ref.at[pl.ds(1, 1)], rgs, p_s.at[1], p_r.at[1], pair)
    first.start()
    second.start()
    first.wait_recv()
    total[...] = lb_ref[0:1, :] + rlb[...]
    out = []
    for shift in range(1, n):
        out.append(copy(total, rbuf.at[shift], g_s.at[shift], g_r.at[shift], mate(shift)))
        out[-1].start()
    second.wait_recv()
    mine = gs_ref[0:1, :]
    theirs = rgs[...]
    steer_out[:, :QCOLS] = jnp.where(a == 0, mine, theirs)
    steer_out[:, QCOLS:] = jnp.where(a == 0, theirs, mine)
    result = total[...]
    for shift in range(1, n):
        out[shift - 1].wait_recv()
        result = result + rbuf[shift]
    bias_out[...] = result
    first.wait_send()
    second.wait_send()
    for one in out:
        one.wait_send()


def reduce(gs, lb):
    ql = lb.shape[1]
    return pl.pallas_call(
        reduce_kernel,
        out_shape=(jax.ShapeDtypeStruct((1, 2 * QCOLS), F32), jax.ShapeDtypeStruct((1, ql), F32)),
        in_specs=[VM, VM],
        out_specs=[VM, VM],
        scratch_shapes=[
            pltpu.VMEM((1, ql), F32),
            pltpu.VMEM((16, 1, ql), F32),
            pltpu.VMEM((1, QCOLS), F32),
            pltpu.VMEM((1, ql), F32),
            pltpu.SemaphoreType.DMA((2,)),
            pltpu.SemaphoreType.DMA((2,)),
            pltpu.SemaphoreType.DMA((16,)),
            pltpu.SemaphoreType.DMA((16,)),
        ],
        compiler_params=pltpu.CompilerParams(collective_id=1, has_side_effects=True),
        name="reduce",
    )(gs, lb)


def shards(
    q_latent, latent_bias, norm_gain, w_q, steer, kv_latent, key_rope, w_uk, w_uv, d_out, block_mask
):
    ql = q_latent.shape[1]
    W, KV, Xq, Xb, Xs, Xd = gather(w_q, q_latent, latent_bias, steer, d_out, kv_latent, key_rope)
    gs, lb = attend(
        block_mask, q_latent, Xq, latent_bias, Xb, norm_gain, W.reshape(2, ql, QTWO), steer, Xs,
        KV, w_uk, w_uv, d_out, Xd,
    )
    grad_steer, grad_bias = reduce(gs, lb)
    return (grad_steer, grad_bias)


def solution(mesh):
    in_specs = (
        P("ctx", None),
        P("ctx", None),
        P(),
        P("ctx", "head"),
        P("ctx", "head"),
        P("ctx", None),
        P("ctx", None),
        P(None, "head"),
        P(None, "head"),
        P("ctx", "head"),
        P(),
    )
    out_specs = (P("ctx", "head"), P("ctx", None))
    return jax.shard_map(shards, mesh=mesh, in_specs=in_specs, out_specs=out_specs, check_vma=False)
```

```python
import functools
import math

import jax
import jax.numpy as jnp
from jax import lax
from jax.experimental import pallas as pl
from jax.experimental.pallas import tpu as pltpu
from jax.sharding import PartitionSpec as P

KVL = 512
NOPE = 128
ROPE = 64
BLK = 128
WIDE = 640
HALF = 4
HEADW = NOPE + ROPE
QCOLS = HALF * HEADW
QTWO = QCOLS // 2
DCOLS = HALF * NOPE
EPS = 1e-06
LOWEST = -1e30
NZ = 16
NY = 4
MESH = pl.DeviceIdType.MESH
F32 = jnp.float32
BF16 = jnp.bfloat16
ANY = pl.BlockSpec(memory_space=pl.ANY)
HBM = pl.BlockSpec(memory_space=pltpu.HBM)
VM = pl.BlockSpec(memory_space=pltpu.VMEM)


def last_last(left, right):
    return lax.dot_general(left, right, (((1,), (1,)), ((), ())), preferred_element_type=F32)


def place():
    c = lax.axis_index("ctx")
    k = lax.axis_index("head")
    return c, k, c // NZ, lax.rem(c, NZ)


def gather_kernel(
    w_ref, q_ref, b_ref, s_ref, d_ref, kv_ref, kr_ref,
    W, KV, Xq, Xb, Xs, Xd,
    own, rope,
    w_s, w_r, z_s, z_r, y_s, y_r, f_s, f_r, x_s, x_r, c_s, c_r, m_s, m_r, loc,
):
    c, k, a, z = place()
    x_hi = k // 8
    y = lax.rem(k, 8) // 2
    core = lax.rem(k, 2)
    z_right = (a * NZ + lax.rem(z + 1, NZ), k)
    z_left = (a * NZ + lax.rem(z + NZ - 1, NZ), k)
    z_right2 = (a * NZ + lax.rem(z + 2, NZ), k)
    z_left2 = (a * NZ + lax.rem(z + NZ - 2, NZ), k)
    y_right = (c, x_hi * 8 + lax.rem(y + 1, NY) * 2 + core)
    y_left = (c, x_hi * 8 + lax.rem(y + NY - 1, NY) * 2 + core)
    sibling = (c, x_hi * 8 + y * 2 + (1 - core))
    pair = ((1 - a) * NZ + z, k)
    across = ((1 - a) * NZ + z, (1 - x_hi) * 8 + y * 2 + core)

    barrier = pltpu.get_barrier_semaphore()
    for dev in (z_right, z_left, z_right2, z_left2, y_right, y_left, sibling, pair, across):
        pl.semaphore_signal(barrier, inc=1, device_id=dev, device_id_type=MESH)

    load_k = pltpu.make_async_copy(kv_ref, own.at[:, pl.ds(0, KVL)], loc.at[2])
    load_r = pltpu.make_async_copy(kr_ref, rope, loc.at[3])
    load_k.start()
    load_r.start()
    load_r.wait()
    tall = jnp.concatenate([rope[...].astype(F32), jnp.zeros((WIDE - KVL - ROPE, BLK), F32)], axis=0)
    own[:, KVL:] = tall.T.astype(BF16)
    load_k.wait()
    pl.semaphore_wait(barrier, 9)

    sends = []

    def send(src, dst, s, r, dev):
        copy = pltpu.make_async_remote_copy(
            src_ref=src, dst_ref=dst, send_sem=s, recv_sem=r, device_id=dev, device_id_type=MESH
        )
        copy.start()
        sends.append(copy)

    def got(dst, s, r):
        pltpu.make_async_remote_copy(
            src_ref=dst, dst_ref=dst, send_sem=s, recv_sem=r, device_id=pair, device_id_type=MESH
        ).wait_recv()

    def columns(who, two):
        return pl.ds(pl.multiple_of(who * QCOLS + two * QTWO, 128), QTWO)

    their_d = pl.ds(pl.multiple_of((1 - a) * DCOLS, 128), DCOLS)

    counts = {(0, 0): 8, (0, 1): 7, (1, 0): 7, (1, 1): 8}

    def w_slot(part, two, zz):
        return W.at[two, (a if part == 0 else 1 - a) * NZ + lax.rem(zz + 2 * NZ, NZ)]

    def w_send(way, part, two, step):
        at = z - (step - 1) if way == 0 else z + (step - 1)
        slot = w_slot(part, two, at)
        src = w_ref.at[:, columns(a, two)] if step == 1 and part == 0 else slot
        n = 4 * way + 2 * part + two
        send(src, slot, w_s.at[n, step - 1], w_r.at[n, step - 1], z_left if way else z_right)

    def w(step):
        for part, two in ((0, 0), (0, 1), (1, 0), (1, 1)):
            for way in (0, 1):
                if step <= counts[way, part]:
                    n = 4 * way + 2 * part + two
                    at = z + step if way else z - step
                    got(w_slot(part, two, at), w_s.at[n, step - 1], w_r.at[n, step - 1])
                    if step + 1 <= counts[way, part]:
                        w_send(way, part, two, step + 1)

    rows = pl.ds(pl.multiple_of(core * 64 + y * 16, 16), 16)

    def far(way, step):
        return 0 if step == 0 else (2 * step if way else 2 * step - 1)

    def z_send(way, step):
        hop = 1 if step == 1 else 2
        src = own.at[rows] if step <= 2 else KV.at[a, far(way, step - 2), rows]
        dev = (z_left if way else z_right) if hop == 1 else (z_left2 if way else z_right2)
        send(src, KV.at[a, far(way, step), rows], z_s.at[way, step - 1], z_r.at[way, step - 1], dev)

    def kz(step):
        for way in range(2):
            if step <= 8 - way:
                got(KV.at[a, far(way, step), rows], z_s.at[way, step - 1], z_r.at[way, step - 1])
                if step + 2 <= 8 - way:
                    z_send(way, step + 2)

    def y_rows(shift):
        return pl.ds(pl.multiple_of(core * 64 + lax.rem(y + shift + NY, NY) * 16, 16), 16)

    def block(far_side, first, count, row):
        return KV.at[1 - a if far_side else a, pl.ds(first, count), row]

    def kx(q):
        for n, dev in ((0, pair), (1, across)):
            part = block(0, 4 * q + 2 * n, 2, rows)
            send(part, part, x_s.at[n, q], x_r.at[n, q], dev)

    def ky(q, far_side):
        if far_side:
            for n in range(2):
                got(block(1, 4 * q + 2 * n, 2, rows), x_s.at[n, q], x_r.at[n, q])
        part = block(far_side, 4 * q, 4, rows)
        for way in range(2):
            n = 2 * far_side + way
            send(part, part, y_s.at[n, q], y_r.at[n, q], y_left if way else y_right)

    def kf(q, far_side):
        for way in range(2):
            n = 2 * far_side + way
            row = y_rows(1 if way else -1)
            got(block(far_side, 4 * q, 4, row), y_s.at[n, q], y_r.at[n, q])
            part = block(far_side, 4 * q + 2 * way, 2, row)
            send(part, part, f_s.at[n, q], f_r.at[n, q], y_left if way else y_right)

    half = pl.ds(pl.multiple_of(core * 64, 16), 64)

    def kc(q):
        for far_side in range(2):
            for way in range(2):
                n = 2 * far_side + way
                got(block(far_side, 4 * q + 2 * way, 2, y_rows(2)), f_s.at[n, q], f_r.at[n, q])
        part = KV.at[:, pl.ds(4 * q, 4), half]
        send(part, part, c_s.at[q], c_r.at[q], sibling)

    for two in range(2):
        send(w_ref.at[:, columns(1 - a, two)], W.at[two, c], m_s.at[6 * two], m_r.at[6 * two], pair)
    for step in (1, 2):
        z_send(0, step)
        z_send(1, step)
    for two in range(2):
        w_send(0, 0, two, 1)
        w_send(1, 0, two, 1)
    copy_w = [pltpu.make_async_copy(w_ref.at[:, columns(a, two)], W.at[two, c], loc.at[4 * two]) for two in range(2)]
    for copy in copy_w:
        copy.start()
    copy_k = pltpu.make_async_copy(own.at[rows], KV.at[a, 0, rows], loc.at[1])
    copy_k.start()
    q_rows = pl.ds(pl.multiple_of(core * 64, 16), 64)
    send(q_ref.at[q_rows], Xq.at[q_rows], m_s.at[1], m_r.at[1], pair)
    send(d_ref.at[:, their_d], Xd, m_s.at[3], m_r.at[3], pair)
    send(b_ref, Xb, m_s.at[4], m_r.at[4], pair)
    send(s_ref, Xs, m_s.at[5], m_r.at[5], pair)
    for two in range(2):
        got(w_slot(1, two, z), m_s.at[6 * two], m_r.at[6 * two])
        w_send(0, 1, two, 1)
        w_send(1, 1, two, 1)

    kz(1)
    kz(2)
    copy_k.wait()
    kx(0)
    ky(0, 0)
    w(1)
    kz(3)
    ky(0, 1)
    kz(4)
    kx(1)
    ky(1, 0)
    kf(0, 0)
    w(2)
    kz(5)
    ky(1, 1)
    kz(6)
    kx(2)
    ky(2, 0)
    kf(0, 1)
    kf(1, 0)
    w(3)
    kz(7)
    ky(2, 1)
    kz(8)
    kx(3)
    ky(3, 0)
    kf(1, 1)
    kf(2, 0)
    w(4)
    kc(0)
    ky(3, 1)
    got(Xq.at[q_rows], m_s.at[1], m_r.at[1])
    send(Xq.at[q_rows], Xq.at[q_rows], m_s.at[2], m_r.at[2], sibling)
    kf(2, 1)
    kf(3, 0)
    w(5)
    kc(1)
    w(6)
    kf(3, 1)
    kc(2)
    w(7)
    kc(3)
    w(8)

    other = pl.ds(pl.multiple_of((1 - core) * 64, 16), 64)
    for q in range(4):
        got(KV.at[:, pl.ds(4 * q, 4), other], c_s.at[q], c_r.at[q])
    got(Xq.at[other], m_s.at[2], m_r.at[2])
    got(Xd, m_s.at[3], m_r.at[3])
    got(Xb, m_s.at[4], m_r.at[4])
    got(Xs, m_s.at[5], m_r.at[5])
    for copy in copy_w:
        copy.wait()
    for copy in sends:
        copy.wait_send()


def gather(w_q, q_latent, latent_bias, steer, d_out, kv_latent, key_rope):
    def dma(*shape):
        return pltpu.SemaphoreType.DMA(shape)

    return pl.pallas_call(
        gather_kernel,
        out_shape=(
            jax.ShapeDtypeStruct((2, 2 * NZ, w_q.shape[0], QTWO), BF16),
            jax.ShapeDtypeStruct((2, NZ, BLK, WIDE), BF16),
            jax.ShapeDtypeStruct(q_latent.shape, BF16),
            jax.ShapeDtypeStruct(latent_bias.shape, F32),
            jax.ShapeDtypeStruct(steer.shape, F32),
            jax.ShapeDtypeStruct((BLK, DCOLS), BF16),
        ),
        in_specs=[HBM] * 7,
        out_specs=[ANY] * 6,
        scratch_shapes=[
            pltpu.VMEM((BLK, WIDE), BF16),
            pltpu.VMEM((ROPE, BLK), BF16),
            dma(8, 8), dma(8, 8), dma(2, 8), dma(2, 8), dma(4, 4), dma(4, 4), dma(4, 4), dma(4, 4),
            dma(2, 4), dma(2, 4), dma(4), dma(4), dma(7), dma(7), dma(5),
        ],
        compiler_params=pltpu.CompilerParams(
            collective_id=0, has_side_effects=True, vmem_limit_bytes=54 * 2**20
        ),
        cost_estimate=pl.CostEstimate(flops=0, bytes_accessed=20_000_000, transcendentals=0),
        name="gather",
    )(w_q, q_latent, latent_bias, steer, d_out, kv_latent, key_rope)


CHUNK = 256
TILES = CHUNK // BLK


def attend_kernel(
    mask, q_ref, xq_ref, b_ref, xb_ref, gain_ref, W_ref, s_ref, xs_ref, KV, uk_ref, uv_ref, d_ref, xd_ref,
    gs_ref, lb_ref,
    Wv, q2, uk, uv, dv, keys_all, cq, pj, qg, qr, sbuf, dbuf, acc, gl, gr, peak, lsum, gsum, u_ref,
    index, sem,
):
    c, k, a, z = place()
    gain = gain_ref[...].reshape(1, gain_ref.shape[0])
    scale = HEADW ** (-0.5)
    scale2 = scale * math.log2(math.e)
    rows = HALF * BLK
    my_d = pl.ds(pl.multiple_of(a * DCOLS, 128), DCOLS)
    loads = [
        pltpu.make_async_copy(q_ref, q2.at[0], sem.at[0]),
        pltpu.make_async_copy(W_ref, Wv, sem.at[1]),
        pltpu.make_async_copy(uk_ref.at[:, my_d], uk, sem.at[2]),
        pltpu.make_async_copy(uv_ref.at[:, my_d], uv, sem.at[3]),
        pltpu.make_async_copy(d_ref.at[:, my_d], dv.at[0], sem.at[4]),
        pltpu.make_async_copy(xq_ref, q2.at[1], sem.at[5]),
        pltpu.make_async_copy(xd_ref, dv.at[1], sem.at[6]),
        pltpu.make_async_copy(KV, keys_all, sem.at[7]),
    ]
    for copy in loads:
        copy.start()

    live = []
    for i in range(2):
        block = c if i == 0 else lax.rem(c + NZ, 2 * NZ)

        def visit(j, n):
            far = lax.rem(z - lax.rem(j, NZ) + NZ, NZ)
            slot = jnp.where(far == 0, 0, jnp.where(far <= NZ // 2, 2 * far - 1, 2 * (NZ - far)))
            index[i, n] = (j // NZ) * NZ + slot
            return n + jnp.where(mask[block, j] > 0, 1, 0)

        n = lax.fori_loop(0, 2 * NZ, visit, 0)
        for extra in range(TILES - 1):
            index[i, n + extra] = 0
        live.append(n)

    def chunks_of(n):
        return (n + TILES - 1) // TILES

    def keys_of(i, t):
        return jnp.concatenate([keys_all[index[i, t * TILES + d]] for d in range(TILES)], axis=0)

    invs = []
    for i in range(2):
        loads[5 * i].wait()
        shifted = q2[i].astype(F32) + (b_ref, xb_ref)[i][...]
        invs.append(lax.rsqrt(jnp.mean(shifted * shifted, axis=1, keepdims=True) + EPS))
        cq[i] = (shifted * invs[i] * gain).astype(BF16)
    both = 2 * BLK
    loads[3].wait()
    loads[4].wait()
    loads[6].wait()
    for h in range(HALF):
        up = slice(h * NOPE, (h + 1) * NOPE)
        g = last_last(dv[:, :, up].reshape(both, NOPE), uv[:, up]).astype(BF16)
        for i in range(2):
            qg[i, rows + h * BLK : rows + (h + 1) * BLK, :] = g[i * BLK : (i + 1) * BLK]
    loads[1].wait()
    loads[2].wait()
    c_query = cq[...].reshape(both, cq.shape[2])
    for two in range(2):
        proj = jnp.dot(c_query, Wv[two], preferred_element_type=F32)
        pj[:, two * QTWO : (two + 1) * QTWO] = proj
        for i in range(2):
            row = (s_ref, xs_ref)[i]
            part = slice(two * QTWO, (two + 1) * QTWO)
            other = slice(QCOLS + two * QTWO, QCOLS + (two + 1) * QTWO)
            cq[i, :, part] = (proj[i * BLK : (i + 1) * BLK] + jnp.where(a == 0, row[:, part], row[:, other])).astype(BF16)
    query = cq[:, :, :QCOLS].reshape(both, QCOLS)
    for h in range(HALF):
        at = h * HEADW
        q = last_last(query[:, at : at + NOPE], uk[:, h * NOPE : (h + 1) * NOPE]).astype(BF16)
        rope = query[:, at + NOPE : at + HEADW]
        rope = jnp.concatenate([rope, jnp.zeros((both, WIDE - KVL - ROPE), BF16)], axis=1)
        for i in range(2):
            qg[i, h * BLK : (h + 1) * BLK, :] = q[i * BLK : (i + 1) * BLK]
            qr[i, h * BLK : (h + 1) * BLK, :] = rope[i * BLK : (i + 1) * BLK]

    def in_fours(count, step):
        def four(t, _):
            step(4 * t, 4)
            return 0

        lax.fori_loop(0, count // 4, four, 0)
        rest = lax.rem(count, 4)

        @pl.when(rest >= 2)
        def _():
            step(count - rest, 2)

        @pl.when(lax.rem(rest, 2) == 1)
        def _():
            step(count - 1, 1)

    def in_pairs(count, step):
        def pair(t, _):
            step(2 * t, 2)
            return 0

        lax.fori_loop(0, count // 2, pair, 0)

        @pl.when(lax.rem(count, 2) == 1)
        def _():
            step(count - 1, 1)

    for i in range(2):
        n = live[i]
        count = chunks_of(n)

        if i == 0:
            loads[7].wait()
        peak[...] = jnp.full((rows, 128), LOWEST, F32)
        lsum[...] = jnp.zeros((rows, 128), F32)
        gsum[...] = jnp.zeros((rows, 128), F32)
        acc[...] = jnp.zeros((rows, WIDE), F32)

        def scores(first, many):
            top = peak[...]
            for t in [first + d for d in range(many)]:
                keys = keys_of(i, t)
                column = lax.broadcasted_iota(jnp.int32, (1, CHUNK), 1) + t * CHUNK
                dead = jnp.where(column < n * BLK, 0.0, LOWEST)
                main = last_last(qg[i], keys[:, :KVL])
                s = main[:rows] + last_last(qr[i], keys[:, KVL:]) + dead
                sbuf[t] = s
                dbuf[t] = main[rows:]
                for part in range(TILES):
                    top = jnp.maximum(top, s[:, part * 128 : (part + 1) * 128])
            peak[...] = top

        in_pairs(count, scores)
        top = jnp.max(peak[...], axis=1, keepdims=True) * scale2

        def weigh(first, many):
            low = lsum[...]
            gow = gsum[...]
            for t in [first + d for d in range(many)]:
                e = jnp.exp2(sbuf[t] * scale2 - top)
                sbuf[t] = e
                mixed = e * dbuf[t]
                low = low + sum(e[:, p * 128 : (p + 1) * 128] for p in range(TILES))
                gow = gow + sum(mixed[:, p * 128 : (p + 1) * 128] for p in range(TILES))
            lsum[...] = low
            gsum[...] = gow

        in_pairs(count, weigh)
        total = jnp.sum(lsum[...], axis=1, keepdims=True)
        ratio = jnp.sum(gsum[...], axis=1, keepdims=True) / total

        def collect(first, many):
            weight = jnp.concatenate(
                [(sbuf[first + d] * (dbuf[first + d] - ratio)).astype(BF16) for d in range(many)], axis=1
            )
            keys = jnp.concatenate([keys_of(i, first + d) for d in range(many)], axis=0)
            acc[...] += jnp.dot(weight, keys, preferred_element_type=F32)

        in_fours(count, collect)
        grad = acc[...] * (scale / total)
        gl[i] = grad[:, :KVL].astype(BF16).reshape(HALF, BLK, KVL)
        gr[i] = grad[:, KVL:].reshape(HALF, BLK, WIDE - KVL)

    pieces = []
    for h in range(HALF):
        pieces.append(
            jnp.dot(gl[:, h].reshape(both, KVL), uk[:, h * NOPE : (h + 1) * NOPE], preferred_element_type=F32)
        )
        pieces.append(gr[:, h].reshape(both, WIDE - KVL)[:, :ROPE])
    all_grads = jnp.concatenate(pieces, axis=1)
    for i in range(2):
        grad_query = all_grads[i * BLK : (i + 1) * BLK]
        gs_ref[i : i + 1, :] = jnp.sum(grad_query, axis=0, keepdims=True)
        lean = jnp.sum(grad_query * pj[i * BLK : (i + 1) * BLK, :], axis=1, keepdims=True)
        u = jnp.sum(grad_query * invs[i], axis=0, keepdims=True)
        u_high = u.astype(BF16)
        u_ref[2 * i : 2 * i + 1, :] = u_high.astype(F32)
        u_ref[2 * i + 1 : 2 * i + 2, :] = u - u_high.astype(F32)
        shifted = q2[i].astype(F32) + (b_ref, xb_ref)[i][...]
        lb_ref[i : i + 1, :] = jnp.sum(shifted * (invs[i] * invs[i] * lean), axis=0, keepdims=True)

    back = sum(
        last_last(u_ref[:, two * QTWO : (two + 1) * QTWO].astype(BF16), Wv[two]) for two in range(2)
    )
    for i in range(2):
        whole = back[2 * i : 2 * i + 1] + back[2 * i + 1 : 2 * i + 2]
        lb_ref[i : i + 1, :] = gain * whole - lb_ref[i : i + 1, :] * (1.0 / gain.shape[1])


def attend(mask, q, xq, b, xb, gain, W, s, xs, KV, w_uk, w_uv, d, xd):
    ql = q.shape[1]
    rows = HALF * BLK
    nchunk = 2 * NZ // TILES
    return pl.pallas_call(
        attend_kernel,
        out_shape=(jax.ShapeDtypeStruct((2, QCOLS), F32), jax.ShapeDtypeStruct((2, ql), F32)),
        in_specs=[
            pl.BlockSpec(memory_space=pltpu.SMEM), HBM, ANY, VM, VM, VM, ANY, VM, VM, ANY, HBM, HBM, HBM, ANY,
        ],
        out_specs=[VM, VM],
        scratch_shapes=[
            pltpu.VMEM((2, ql, QTWO), BF16),
            pltpu.VMEM((2, BLK, ql), BF16),
            pltpu.VMEM((KVL, DCOLS), BF16),
            pltpu.VMEM((KVL, DCOLS), BF16),
            pltpu.VMEM((2, BLK, DCOLS), BF16),
            pltpu.VMEM((2 * NZ, BLK, WIDE), BF16),
            pltpu.VMEM((2, BLK, ql), BF16),
            pltpu.VMEM((2 * BLK, QCOLS), F32),
            pltpu.VMEM((2, 2 * rows, KVL), BF16),
            pltpu.VMEM((2, rows, WIDE - KVL), BF16),
            pltpu.VMEM((nchunk, rows, CHUNK), F32),
            pltpu.VMEM((nchunk, rows, CHUNK), F32),
            pltpu.VMEM((rows, WIDE), F32),
            pltpu.VMEM((2, HALF, BLK, KVL), BF16),
            pltpu.VMEM((2, HALF, BLK, WIDE - KVL), F32),
            pltpu.VMEM((rows, 128), F32),
            pltpu.VMEM((rows, 128), F32),
            pltpu.VMEM((rows, 128), F32),
            pltpu.VMEM((16, QCOLS), F32),
            pltpu.SMEM((2, 2 * NZ + TILES), jnp.int32),
            pltpu.SemaphoreType.DMA((8,)),
        ],
        compiler_params=pltpu.CompilerParams(vmem_limit_bytes=54 * 2**20),
        cost_estimate=pl.CostEstimate(flops=10_000_000_000, bytes_accessed=10_000_000, transcendentals=4_000_000),
        name="attend",
    )(mask, q, xq, b, xb, gain, W, s, xs, KV, w_uk, w_uv, d, xd)


def reduce_kernel(gs_ref, lb_ref, steer_out, bias_out, rbuf, rgs, p_s, p_r, g_s, g_r):
    c, k, a, z = place()
    pair_c = (1 - a) * NZ + z
    n = 16

    def mate(side, shift):
        return (pair_c if side else c, lax.rem(k + shift, n))

    others = [(side, shift) for side in range(2) for shift in range(n) if side or shift]
    barrier = pltpu.get_barrier_semaphore()
    for one in others:
        pl.semaphore_signal(barrier, inc=1, device_id=mate(*one), device_id_type=MESH)
    pl.semaphore_wait(barrier, len(others))

    def copy(src, dst, s, r, dev):
        return pltpu.make_async_remote_copy(
            src_ref=src, dst_ref=dst, send_sem=s, recv_sem=r, device_id=dev, device_id_type=MESH
        )

    steer_copy = copy(gs_ref.at[pl.ds(1, 1)], rgs, p_s.at[0], p_r.at[0], mate(1, 0))
    steer_copy.start()
    out = []
    for side, shift in others:
        at = side * n + shift
        out.append(
            copy(lb_ref.at[pl.ds(side, 1)], rbuf.at[at], g_s.at[at], g_r.at[at], mate(side, shift))
        )
        out[-1].start()
    steer_copy.wait_recv()
    mine = gs_ref[0:1, :]
    theirs = rgs[...]
    steer_out[:, :QCOLS] = jnp.where(a == 0, mine, theirs)
    steer_out[:, QCOLS:] = jnp.where(a == 0, theirs, mine)
    result = lb_ref[0:1, :]
    for (side, shift), one in zip(others, out):
        one.wait_recv()
        result = result + rbuf[side * n + shift]
    bias_out[...] = result
    steer_copy.wait_send()
    for one in out:
        one.wait_send()


def reduce(gs, lb):
    ql = lb.shape[1]
    return pl.pallas_call(
        reduce_kernel,
        out_shape=(jax.ShapeDtypeStruct((1, 2 * QCOLS), F32), jax.ShapeDtypeStruct((1, ql), F32)),
        in_specs=[VM, VM],
        out_specs=[VM, VM],
        scratch_shapes=[
            pltpu.VMEM((32, 1, ql), F32),
            pltpu.VMEM((1, QCOLS), F32),
            pltpu.SemaphoreType.DMA((1,)),
            pltpu.SemaphoreType.DMA((1,)),
            pltpu.SemaphoreType.DMA((32,)),
            pltpu.SemaphoreType.DMA((32,)),
        ],
        compiler_params=pltpu.CompilerParams(collective_id=1, has_side_effects=True),
        name="reduce",
    )(gs, lb)


def shards(
    q_latent, latent_bias, norm_gain, w_q, steer, kv_latent, key_rope, w_uk, w_uv, d_out, block_mask
):
    ql = q_latent.shape[1]
    W, KV, Xq, Xb, Xs, Xd = gather(w_q, q_latent, latent_bias, steer, d_out, kv_latent, key_rope.T)
    gs, lb = attend(
        block_mask, q_latent, Xq, latent_bias, Xb, norm_gain, W.reshape(2, ql, QTWO), steer, Xs,
        KV.reshape(2 * NZ, BLK, WIDE), w_uk, w_uv, d_out, Xd,
    )
    grad_steer, grad_bias = reduce(gs, lb)
    return (grad_steer, grad_bias)


def solution(mesh):
    in_specs = (
        P("ctx", None),
        P("ctx", None),
        P(),
        P("ctx", "head"),
        P("ctx", "head"),
        P("ctx", None),
        P("ctx", None),
        P(None, "head"),
        P(None, "head"),
        P("ctx", "head"),
        P(),
    )
    out_specs = (P("ctx", "head"), P("ctx", None))
    return jax.shard_map(shards, mesh=mesh, in_specs=in_specs, out_specs=out_specs, check_vma=False)
```

```python
import functools
import math

import jax
import jax.numpy as jnp
from jax import lax
from jax.experimental import pallas as pl
from jax.experimental.pallas import tpu as pltpu
from jax.sharding import PartitionSpec as P

KVL = 512
NOPE = 128
ROPE = 64
BLK = 128
WIDE = 640
HALF = 4
HEADW = NOPE + ROPE
QCOLS = HALF * HEADW
QTWO = QCOLS // 2
DCOLS = HALF * NOPE
EPS = 1e-06
LOWEST = -1e30
NZ = 16
NY = 4
MESH = pl.DeviceIdType.MESH
F32 = jnp.float32
BF16 = jnp.bfloat16
ANY = pl.BlockSpec(memory_space=pl.ANY)
HBM = pl.BlockSpec(memory_space=pltpu.HBM)
VM = pl.BlockSpec(memory_space=pltpu.VMEM)


def last_last(left, right):
    return lax.dot_general(left, right, (((1,), (1,)), ((), ())), preferred_element_type=F32)


def place():
    c = lax.axis_index("ctx")
    k = lax.axis_index("head")
    return c, k, c // NZ, lax.rem(c, NZ)


def gather_kernel(
    w_ref, q_ref, b_ref, s_ref, d_ref, kv_ref, kr_ref, uk_ref, uv_ref, gain_ref,
    W_out, KV_out, xq_out, xb_out, qg_out, qr_out, pj_out,
    qg, qr, pj, W, KV, own, rope, q2, bv, sv, dv, uk, uv, cq,
    w_s, w_r, z_s, z_r, y_s, y_r, f_s, f_r, x_s, x_r, c_s, c_r, m_s, m_r, loc, fill, drain,
):
    c, k, a, z = place()
    x_hi = k // 8
    y = lax.rem(k, 8) // 2
    core = lax.rem(k, 2)
    z_right = (a * NZ + lax.rem(z + 1, NZ), k)
    z_left = (a * NZ + lax.rem(z + NZ - 1, NZ), k)
    first_hop = 2 - x_hi
    z_first = tuple((a * NZ + lax.rem(z + NZ + way * first_hop, NZ), k) for way in (1, -1))
    z_next = tuple((a * NZ + lax.rem(z + NZ + way * 2, NZ), k) for way in (1, -1))
    y_right = (c, x_hi * 8 + lax.rem(y + 1, NY) * 2 + core)
    y_left = (c, x_hi * 8 + lax.rem(y + NY - 1, NY) * 2 + core)
    sibling = (c, x_hi * 8 + y * 2 + (1 - core))
    pair = ((1 - a) * NZ + z, k)
    across = ((1 - a) * NZ + z, (1 - x_hi) * 8 + y * 2 + core)
    far = (c, (1 - x_hi) * 8 + y * 2 + core)

    barrier = pltpu.get_barrier_semaphore()
    for dev in (z_right, z_left, *z_first, *z_next, y_right, y_left, sibling, pair, across, far):
        pl.semaphore_signal(barrier, inc=1, device_id=dev, device_id_type=MESH)

    my_d = pl.ds(pl.multiple_of(a * DCOLS, 128), DCOLS)
    fills = [
        pltpu.make_async_copy(q_ref, q2.at[0], fill.at[0]),
        pltpu.make_async_copy(b_ref, bv.at[0], fill.at[1]),
        pltpu.make_async_copy(s_ref, sv.at[0], fill.at[2]),
        pltpu.make_async_copy(d_ref.at[:, my_d], dv.at[0], fill.at[3]),
        pltpu.make_async_copy(uk_ref.at[:, my_d], uk, fill.at[4]),
        pltpu.make_async_copy(uv_ref.at[:, my_d], uv, fill.at[5]),
    ]
    load_k = pltpu.make_async_copy(kv_ref, own.at[:, pl.ds(0, KVL)], loc.at[2])
    load_r = pltpu.make_async_copy(kr_ref, rope, loc.at[3])
    load_k.start()
    load_r.start()
    load_r.wait()
    tall = jnp.concatenate([rope[...].astype(F32), jnp.zeros((WIDE - KVL - ROPE, BLK), F32)], axis=0)
    own[:, KVL:] = tall.T.astype(BF16)
    load_k.wait()
    for copy in fills:
        copy.start()
    pl.semaphore_wait(barrier, 12)

    sends = []

    def send(src, dst, s, r, dev):
        copy = pltpu.make_async_remote_copy(
            src_ref=src, dst_ref=dst, send_sem=s, recv_sem=r, device_id=dev, device_id_type=MESH
        )
        copy.start()
        sends.append(copy)

    def got(dst, s, r):
        pltpu.make_async_remote_copy(
            src_ref=dst, dst_ref=dst, send_sem=s, recv_sem=r, device_id=pair, device_id_type=MESH
        ).wait_recv()

    def columns(who, two):
        return pl.ds(pl.multiple_of(who * QCOLS + two * QTWO, 128), QTWO)

    their_d = pl.ds(pl.multiple_of((1 - a) * DCOLS, 128), DCOLS)

    counts = {(0, 0): 8, (0, 1): 7, (1, 0): 7, (1, 1): 8}

    def w_slot(part, two, zz):
        return W.at[two, (a if part == 0 else 1 - a) * NZ + lax.rem(zz + 2 * NZ, NZ)]

    def w_send(way, part, two, step):
        at = z - (step - 1) if way == 0 else z + (step - 1)
        slot = w_slot(part, two, at)
        src = w_ref.at[:, columns(a, two)] if step == 1 and part == 0 else slot
        n = 4 * way + 2 * part + two
        send(src, slot, w_s.at[n, step - 1], w_r.at[n, step - 1], z_left if way else z_right)

    def w(step):
        for part, two in ((0, 0), (0, 1), (1, 0), (1, 1)):
            for way in (0, 1):
                if step <= counts[way, part]:
                    n = 4 * way + 2 * part + two
                    at = z + step if way else z - step
                    got(w_slot(part, two, at), w_s.at[n, step - 1], w_r.at[n, step - 1])
                    if step + 1 <= counts[way, part]:
                        w_send(way, part, two, step + 1)

    rows = pl.ds(pl.multiple_of(core * 64 + y * 16, 16), 16)

    def z_slot(way, step):
        at = jnp.where(x_hi == 0, 2 * step - 1, 2 * step - 2) + way
        return KV.at[at // 2, a, x_hi, lax.rem(at, 2), rows]

    def z_send(way, step):
        src = own.at[rows] if step == 1 else z_slot(way, step - 1)
        dev = (z_first if step == 1 else z_next)[way]
        send(src, z_slot(way, step), z_s.at[way, step - 1], z_r.at[way, step - 1], dev)

    def kz(step):
        def one(way):
            got(z_slot(way, step), z_s.at[way, step - 1], z_r.at[way, step - 1])

        one(0)
        if step < 4:
            z_send(0, step + 1)
            one(1)
            if step < 3:
                z_send(1, step + 1)
            else:
                pl.when(x_hi == 1)(lambda: last_left().start())
        else:
            pl.when(x_hi == 1)(lambda: one(1))

    def last_left():
        return pltpu.make_async_remote_copy(
            src_ref=KV.at[2, a, 1, 1, rows], dst_ref=KV.at[3, a, 1, 1, rows],
            send_sem=z_s.at[1, 3], recv_sem=z_r.at[1, 3], device_id=z_next[1], device_id_type=MESH,
        )

    def y_rows(shift):
        return pl.ds(pl.multiple_of(core * 64 + lax.rem(y + shift + NY, NY) * 16, 16), 16)

    def kx(q):
        part = KV.at[q, a, x_hi, :, rows]
        for n, dev in ((0, far), (1, across), (2, pair)):
            send(part, part, x_s.at[n, q], x_r.at[n, q], dev)

    def ky(q):
        for n, side, parity in ((2, 1 - a, x_hi), (1, 1 - a, 1 - x_hi), (0, a, 1 - x_hi)):
            got(KV.at[q, side, parity, :, rows], x_s.at[n, q], x_r.at[n, q])
        part = KV.at[q, :, :, :, rows]
        for way in range(2):
            send(part, part, y_s.at[way, q], y_r.at[way, q], y_left if way else y_right)

    def kf(q):
        for way in range(2):
            row = y_rows(1 if way else -1)
            got(KV.at[q, :, :, :, row], y_s.at[way, q], y_r.at[way, q])
            part = KV.at[q, way, :, :, row]
            send(part, part, f_s.at[way, q], f_r.at[way, q], y_left if way else y_right)

    half = pl.ds(pl.multiple_of(core * 64, 16), 64)

    def kc(q):
        for way in range(2):
            got(KV.at[q, way, :, :, y_rows(2)], f_s.at[way, q], f_r.at[way, q])
        part = KV.at[q, :, :, :, half]
        send(part, part, c_s.at[q], c_r.at[q], sibling)

    for two in range(2):
        send(w_ref.at[:, columns(1 - a, two)], W.at[two, c], m_s.at[6 * two], m_r.at[6 * two], pair)
    z_send(0, 1)
    z_send(1, 1)
    for two in range(2):
        w_send(0, 0, two, 1)
        w_send(1, 0, two, 1)
    copy_w = [pltpu.make_async_copy(w_ref.at[:, columns(a, two)], W.at[two, c], loc.at[4 * two]) for two in range(2)]
    for copy in copy_w:
        copy.start()
    copy_k = pltpu.make_async_copy(own.at[rows], KV.at[0, a, 0, 0, rows], loc.at[1])
    pl.when(x_hi == 0)(lambda: copy_k.start())
    q_rows = pl.ds(pl.multiple_of(core * 64, 16), 64)
    send(q_ref.at[q_rows], q2.at[1, q_rows], m_s.at[1], m_r.at[1], pair)
    send(d_ref.at[:, their_d], dv.at[1], m_s.at[3], m_r.at[3], pair)
    send(b_ref, bv.at[1], m_s.at[4], m_r.at[4], pair)
    send(s_ref, sv.at[1], m_s.at[5], m_r.at[5], pair)
    for two in range(2):
        got(w_slot(1, two, z), m_s.at[6 * two], m_r.at[6 * two])
        w_send(0, 1, two, 1)
        w_send(1, 1, two, 1)

    both = 2 * BLK
    gain = gain_ref[...].reshape(1, gain_ref.shape[0])

    def norm(i):
        shifted = q2[i].astype(F32) + bv[i]
        inv = lax.rsqrt(jnp.mean(shifted * shifted, axis=1, keepdims=True) + EPS)
        cq[i] = (shifted * inv * gain).astype(BF16)

    def absorb_g(i):
        for h in range(HALF):
            up = slice(h * NOPE, (h + 1) * NOPE)
            qg[i, (HALF + h) * BLK : (HALF + h + 1) * BLK, :] = last_last(dv[i, :, up], uv[:, up]).astype(BF16)

    other = pl.ds(pl.multiple_of((1 - core) * 64, 16), 64)
    drains = []

    def store(src, dst):
        drains.append(pltpu.make_async_copy(src, dst, drain.at[len(drains)]))
        drains[-1].start()

    def kend(q):
        got(KV.at[q, :, :, :, other], c_s.at[q], c_r.at[q])
        store(KV.at[q], KV_out.at[q])

    for copy in fills:
        copy.wait()
    norm(0)
    kz(1)
    pl.when(x_hi == 0)(lambda: copy_k.wait())
    kx(0)
    w(1)
    absorb_g(0)
    kz(2)
    kx(1)
    ky(0)
    w(2)
    kz(3)
    kx(2)
    kf(0)
    ky(1)
    got(q2.at[1, q_rows], m_s.at[1], m_r.at[1])
    send(q2.at[1, q_rows], q2.at[1, q_rows], m_s.at[2], m_r.at[2], sibling)
    w(3)
    kz(4)
    kx(3)
    kf(1)
    ky(2)
    kc(0)
    w(4)
    got(q2.at[1, other], m_s.at[2], m_r.at[2])
    got(dv.at[1], m_s.at[3], m_r.at[3])
    got(bv.at[1], m_s.at[4], m_r.at[4])
    got(sv.at[1], m_s.at[5], m_r.at[5])
    store(q2.at[1], xq_out)
    store(bv.at[1], xb_out)
    norm(1)
    ky(3)
    kf(2)
    kc(1)
    w(5)
    absorb_g(1)
    store(qg.at[:, pl.ds(HALF * BLK, HALF * BLK)], qg_out.at[:, pl.ds(HALF * BLK, HALF * BLK)])
    kend(0)
    kf(3)
    w(6)
    kc(2)
    kend(1)
    w(7)
    kc(3)
    kend(2)
    w(8)
    kend(3)
    for copy in copy_w:
        copy.wait()
    store(W, W_out)
    c_query = cq[...].reshape(both, cq.shape[2])
    for two in range(2):
        weights = W[two].reshape(cq.shape[2], QTWO)
        proj = jnp.dot(c_query, weights, preferred_element_type=F32)
        pj[two] = proj
        store(pj.at[two], pj_out.at[two])
        query = []
        for i in range(2):
            row = sv[i]
            part = slice(two * QTWO, (two + 1) * QTWO)
            rest = slice(QCOLS + two * QTWO, QCOLS + (two + 1) * QTWO)
            query.append(proj[i * BLK : (i + 1) * BLK] + jnp.where(a == 0, row[:, part], row[:, rest]))
        query = jnp.concatenate(query, axis=0).astype(BF16)
        for local in range(2):
            h = 2 * two + local
            at = local * HEADW
            q = last_last(query[:, at : at + NOPE], uk[:, h * NOPE : (h + 1) * NOPE]).astype(BF16)
            pos = query[:, at + NOPE : at + HEADW]
            pos = jnp.concatenate([pos, jnp.zeros((both, WIDE - KVL - ROPE), BF16)], axis=1)
            for i in range(2):
                qg[i, h * BLK : (h + 1) * BLK, :] = q[i * BLK : (i + 1) * BLK]
                qr[i, h * BLK : (h + 1) * BLK, :] = pos[i * BLK : (i + 1) * BLK]
        done = pl.ds(2 * two * BLK, 2 * BLK)
        store(qg.at[:, done], qg_out.at[:, done])
    store(qr, qr_out)
    for copy in drains:
        copy.wait()
    pl.when(x_hi == 1)(lambda: last_left().wait_send())
    for copy in sends:
        copy.wait_send()


def gather(w_q, q_latent, latent_bias, steer, d_out, kv_latent, key_rope, w_uk, w_uv, gain):
    def dma(*shape):
        return pltpu.SemaphoreType.DMA(shape)

    ql = q_latent.shape[1]
    rows = HALF * BLK
    w_shape = (2, 2 * NZ, w_q.shape[0], QTWO)
    k_shape = (NZ // 4, 2, 2, 2, BLK, WIDE)
    return pl.pallas_call(
        gather_kernel,
        out_shape=(
            jax.ShapeDtypeStruct(w_shape, BF16),
            jax.ShapeDtypeStruct(k_shape, BF16),
            jax.ShapeDtypeStruct(q_latent.shape, BF16),
            jax.ShapeDtypeStruct(latent_bias.shape, F32),
            jax.ShapeDtypeStruct((2, 2 * rows, KVL), BF16),
            jax.ShapeDtypeStruct((2, rows, WIDE - KVL), BF16),
            jax.ShapeDtypeStruct((2, 2 * BLK, QTWO), F32),
        ),
        in_specs=[HBM] * 9 + [VM],
        out_specs=[HBM] * 7,
        scratch_shapes=[
            pltpu.VMEM((2, 2 * rows, KVL), BF16),
            pltpu.VMEM((2, rows, WIDE - KVL), BF16),
            pltpu.VMEM((2, 2 * BLK, QTWO), F32),
            pltpu.VMEM(w_shape, BF16),
            pltpu.VMEM(k_shape, BF16),
            pltpu.VMEM((BLK, WIDE), BF16),
            pltpu.VMEM((ROPE, BLK), BF16),
            pltpu.VMEM((2, BLK, ql), BF16),
            pltpu.VMEM((2, 1, ql), F32),
            pltpu.VMEM((2, 1, 2 * QCOLS), F32),
            pltpu.VMEM((2, BLK, DCOLS), BF16),
            pltpu.VMEM((KVL, DCOLS), BF16),
            pltpu.VMEM((KVL, DCOLS), BF16),
            pltpu.VMEM((2, BLK, ql), BF16),
            dma(8, 8), dma(8, 8), dma(2, 4), dma(2, 4), dma(2, 4), dma(2, 4), dma(2, 4), dma(2, 4),
            dma(3, 4), dma(3, 4), dma(4), dma(4), dma(7), dma(7), dma(5), dma(6), dma(16),
        ],
        compiler_params=pltpu.CompilerParams(
            collective_id=0, has_side_effects=True, vmem_limit_bytes=54 * 2**20
        ),
        cost_estimate=pl.CostEstimate(flops=2_000_000_000, bytes_accessed=20_000_000, transcendentals=0),
        name="gather",
    )(w_q, q_latent, latent_bias, steer, d_out, kv_latent, key_rope, w_uk, w_uv, gain)


CHUNK = 256
TILES = CHUNK // BLK


def attend_kernel(
    mask, qg_ref, qr_ref, KV, gl, gr, keys_all, qg, qr, sbuf, dbuf, acc, peak, lsum, gsum, index, sem
):
    c, k, a, z = place()
    scale = HEADW ** (-0.5)
    scale2 = scale * math.log2(math.e)
    rows = HALF * BLK
    loads = [
        pltpu.make_async_copy(qg_ref.at[0], qg.at[0], sem.at[0]),
        pltpu.make_async_copy(qr_ref, qr, sem.at[1]),
        pltpu.make_async_copy(KV, keys_all, sem.at[2]),
        pltpu.make_async_copy(qg_ref.at[1], qg.at[1], sem.at[3]),
    ]
    for copy in loads:
        copy.start()

    live = []
    for i in range(2):
        block = c if i == 0 else lax.rem(c + NZ, 2 * NZ)

        def visit(j, n):
            away = lax.rem(z - lax.rem(j, NZ) + NZ, NZ)
            left = away > NZ // 2
            hops = jnp.where(left, NZ - away, away)
            slot = jnp.where(away == 0, 0, jnp.where(left, hops, hops - 1))
            index[i, n] = ((slot // 2 * 2 + j // NZ) * 2 + lax.rem(hops, 2)) * 2 + lax.rem(slot, 2)
            return n + jnp.where(mask[block, j] > 0, 1, 0)

        n = lax.fori_loop(0, 2 * NZ, visit, 0)
        for extra in range(TILES - 1):
            index[i, n + extra] = 0
        live.append(n)

    def chunks_of(n):
        return (n + TILES - 1) // TILES

    def keys_of(i, t):
        return jnp.concatenate([keys_all[index[i, t * TILES + d]] for d in range(TILES)], axis=0)

    def in_fours(count, step):
        def four(t, _):
            step(4 * t, 4)
            return 0

        lax.fori_loop(0, count // 4, four, 0)
        rest = lax.rem(count, 4)

        @pl.when(rest >= 2)
        def _():
            step(count - rest, 2)

        @pl.when(lax.rem(rest, 2) == 1)
        def _():
            step(count - 1, 1)

    def in_pairs(count, step):
        def pair(t, _):
            step(2 * t, 2)
            return 0

        lax.fori_loop(0, count // 2, pair, 0)

        @pl.when(lax.rem(count, 2) == 1)
        def _():
            step(count - 1, 1)

    for i in range(2):
        n = live[i]
        count = chunks_of(n)

        for copy in loads[3 * i : 3 * i + 3]:
            copy.wait()
        peak[...] = jnp.full((rows, 128), LOWEST, F32)
        lsum[...] = jnp.zeros((rows, 128), F32)
        gsum[...] = jnp.zeros((rows, 128), F32)
        acc[...] = jnp.zeros((rows, WIDE), F32)

        def scores(first, many):
            top = peak[...]
            for t in [first + d for d in range(many)]:
                keys = keys_of(i, t)
                column = lax.broadcasted_iota(jnp.int32, (1, CHUNK), 1) + t * CHUNK
                dead = jnp.where(column < n * BLK, 0.0, LOWEST)
                main = last_last(qg[i], keys[:, :KVL])
                s = main[:rows] + last_last(qr[i], keys[:, KVL:]) + dead
                sbuf[t] = s
                dbuf[t] = main[rows:]
                for part in range(TILES):
                    top = jnp.maximum(top, s[:, part * 128 : (part + 1) * 128])
            peak[...] = top

        in_pairs(count, scores)
        top = jnp.max(peak[...], axis=1, keepdims=True) * scale2

        def weigh(first, many):
            low = lsum[...]
            gow = gsum[...]
            for t in [first + d for d in range(many)]:
                e = jnp.exp2(sbuf[t] * scale2 - top)
                sbuf[t] = e
                mixed = e * dbuf[t]
                low = low + sum(e[:, p * 128 : (p + 1) * 128] for p in range(TILES))
                gow = gow + sum(mixed[:, p * 128 : (p + 1) * 128] for p in range(TILES))
            lsum[...] = low
            gsum[...] = gow

        in_pairs(count, weigh)
        total = jnp.sum(lsum[...], axis=1, keepdims=True)
        ratio = jnp.sum(gsum[...], axis=1, keepdims=True) / total

        def collect(first, many):
            weight = jnp.concatenate(
                [(sbuf[first + d] * (dbuf[first + d] - ratio)).astype(BF16) for d in range(many)], axis=1
            )
            keys = jnp.concatenate([keys_of(i, first + d) for d in range(many)], axis=0)
            acc[...] += jnp.dot(weight, keys, preferred_element_type=F32)

        in_fours(count, collect)
        grad = acc[...] * (scale / total)
        gl[i] = grad[:, :KVL].astype(BF16).reshape(HALF, BLK, KVL)
        gr[i] = grad[:, KVL:].reshape(HALF, BLK, WIDE - KVL)


def attend(mask, qg, qr, KV):
    rows = HALF * BLK
    nchunk = 2 * NZ // TILES
    return pl.pallas_call(
        attend_kernel,
        out_shape=(
            jax.ShapeDtypeStruct((2, HALF, BLK, KVL), BF16),
            jax.ShapeDtypeStruct((2, HALF, BLK, WIDE - KVL), F32),
        ),
        in_specs=[pl.BlockSpec(memory_space=pltpu.SMEM), HBM, HBM, HBM],
        out_specs=[VM, VM],
        scratch_shapes=[
            pltpu.VMEM((2 * NZ, BLK, WIDE), BF16),
            pltpu.VMEM((2, 2 * rows, KVL), BF16),
            pltpu.VMEM((2, rows, WIDE - KVL), BF16),
            pltpu.VMEM((nchunk, rows, CHUNK), F32),
            pltpu.VMEM((nchunk, rows, CHUNK), F32),
            pltpu.VMEM((rows, WIDE), F32),
            pltpu.VMEM((rows, 128), F32),
            pltpu.VMEM((rows, 128), F32),
            pltpu.VMEM((rows, 128), F32),
            pltpu.SMEM((2, 2 * NZ + TILES), jnp.int32),
            pltpu.SemaphoreType.DMA((4,)),
        ],
        compiler_params=pltpu.CompilerParams(vmem_limit_bytes=54 * 2**20),
        cost_estimate=pl.CostEstimate(flops=10_000_000_000, bytes_accessed=10_000_000, transcendentals=4_000_000),
        name="attend",
    )(mask, qg, qr, KV)


def reduce_kernel(
    q_ref, xq_ref, b_ref, xb_ref, gain_ref, W_ref, uk_ref, pj_ref, gl_ref, gr_ref,
    steer_out, bias_out,
    q2, Wv, uk, pj, gl, gr, u_ref, gs_ref, lb_ref, rbuf, rgs, p_s, p_r, g_s, g_r, sem,
):
    c, k, a, z = place()
    pair_c = (1 - a) * NZ + z
    n = 16

    def mate(side, shift):
        return (pair_c if side else c, lax.rem(k + shift, n))

    my_d = pl.ds(pl.multiple_of(a * DCOLS, 128), DCOLS)
    loads = [
        pltpu.make_async_copy(gl_ref, gl, sem.at[0]),
        pltpu.make_async_copy(uk_ref.at[:, my_d], uk, sem.at[1]),
        pltpu.make_async_copy(gr_ref, gr, sem.at[2]),
        pltpu.make_async_copy(pj_ref, pj, sem.at[3]),
        pltpu.make_async_copy(q_ref, q2.at[0], sem.at[4]),
        pltpu.make_async_copy(xq_ref, q2.at[1], sem.at[5]),
        pltpu.make_async_copy(W_ref, Wv, sem.at[6]),
    ]
    for load in loads:
        load.start()
    others = [(side, shift) for side in range(2) for shift in range(n) if side or shift]
    barrier = pltpu.get_barrier_semaphore()
    for one in others:
        pl.semaphore_signal(barrier, inc=1, device_id=mate(*one), device_id_type=MESH)
    both = 2 * BLK
    gain = gain_ref[...].reshape(1, gain_ref.shape[0])
    for load in loads:
        load.wait()
    pieces = []
    for h in range(HALF):
        pieces.append(
            jnp.dot(gl[:, h].reshape(both, KVL), uk[:, h * NOPE : (h + 1) * NOPE], preferred_element_type=F32)
        )
        pieces.append(gr[:, h].reshape(both, WIDE - KVL)[:, :ROPE])
    all_grads = jnp.concatenate(pieces, axis=1)
    u_ref[...] = jnp.zeros_like(u_ref)
    for i in range(2):
        shifted = q2[i].astype(F32) + (b_ref, xb_ref)[i][...]
        inv = lax.rsqrt(jnp.mean(shifted * shifted, axis=1, keepdims=True) + EPS)
        grad_query = all_grads[i * BLK : (i + 1) * BLK]
        gs_ref[i : i + 1, :] = jnp.sum(grad_query, axis=0, keepdims=True)
        lean = sum(
            jnp.sum(
                grad_query[:, two * QTWO : (two + 1) * QTWO] * pj[two, i * BLK : (i + 1) * BLK, :], axis=1, keepdims=True
            )
            for two in range(2)
        )
        u = jnp.sum(grad_query * inv, axis=0, keepdims=True)
        u_high = u.astype(BF16)
        u_ref[2 * i : 2 * i + 1, :] = u_high.astype(F32)
        u_ref[2 * i + 1 : 2 * i + 2, :] = u - u_high.astype(F32)
        lb_ref[i : i + 1, :] = jnp.sum(shifted * (inv * inv * lean), axis=0, keepdims=True)

    back = sum(
        last_last(u_ref[:, two * QTWO : (two + 1) * QTWO].astype(BF16), Wv[two]) for two in range(2)
    )
    for i in range(2):
        whole = back[2 * i : 2 * i + 1] + back[2 * i + 1 : 2 * i + 2]
        lb_ref[i : i + 1, :] = gain * whole - lb_ref[i : i + 1, :] * (1.0 / gain.shape[1])
    pl.semaphore_wait(barrier, len(others))

    def copy(src, dst, s, r, dev):
        return pltpu.make_async_remote_copy(
            src_ref=src, dst_ref=dst, send_sem=s, recv_sem=r, device_id=dev, device_id_type=MESH
        )

    steer_copy = copy(gs_ref.at[pl.ds(1, 1)], rgs, p_s.at[0], p_r.at[0], mate(1, 0))
    steer_copy.start()
    out = []
    for side, shift in others:
        at = side * n + shift
        out.append(
            copy(lb_ref.at[pl.ds(side, 1)], rbuf.at[at], g_s.at[at], g_r.at[at], mate(side, shift))
        )
        out[-1].start()
    steer_copy.wait_recv()
    mine = gs_ref[0:1, :]
    theirs = rgs[...]
    steer_out[:, :QCOLS] = jnp.where(a == 0, mine, theirs)
    steer_out[:, QCOLS:] = jnp.where(a == 0, theirs, mine)
    result = lb_ref[0:1, :]
    for (side, shift), one in zip(others, out):
        one.wait_recv()
        result = result + rbuf[side * n + shift]
    bias_out[...] = result
    steer_copy.wait_send()
    for one in out:
        one.wait_send()


def reduce(q, xq, b, xb, gain, W, w_uk, pj, gl, gr):
    ql = q.shape[1]
    return pl.pallas_call(
        reduce_kernel,
        out_shape=(jax.ShapeDtypeStruct((1, 2 * QCOLS), F32), jax.ShapeDtypeStruct((1, ql), F32)),
        in_specs=[HBM, HBM, VM, VM, VM, HBM, HBM, HBM, HBM, HBM],
        out_specs=[VM, VM],
        scratch_shapes=[
            pltpu.VMEM((2, BLK, ql), BF16),
            pltpu.VMEM((2, ql, QTWO), BF16),
            pltpu.VMEM((KVL, DCOLS), BF16),
            pltpu.VMEM((2, 2 * BLK, QTWO), F32),
            pltpu.VMEM((2, HALF, BLK, KVL), BF16),
            pltpu.VMEM((2, HALF, BLK, WIDE - KVL), F32),
            pltpu.VMEM((16, QCOLS), F32),
            pltpu.VMEM((2, QCOLS), F32),
            pltpu.VMEM((2, ql), F32),
            pltpu.VMEM((32, 1, ql), F32),
            pltpu.VMEM((1, QCOLS), F32),
            pltpu.SemaphoreType.DMA((1,)),
            pltpu.SemaphoreType.DMA((1,)),
            pltpu.SemaphoreType.DMA((32,)),
            pltpu.SemaphoreType.DMA((32,)),
            pltpu.SemaphoreType.DMA((7,)),
        ],
        compiler_params=pltpu.CompilerParams(
            collective_id=1, has_side_effects=True, vmem_limit_bytes=54 * 2**20
        ),
        name="reduce",
    )(q, xq, b, xb, gain, W, w_uk, pj, gl, gr)


def shards(
    q_latent, latent_bias, norm_gain, w_q, steer, kv_latent, key_rope, w_uk, w_uv, d_out, block_mask
):
    ql = q_latent.shape[1]
    W, KV, xq, xb, qg, qr, pj = gather(
        w_q, q_latent, latent_bias, steer, d_out, kv_latent, key_rope.T, w_uk, w_uv, norm_gain
    )
    gl, gr = attend(block_mask, qg, qr, KV.reshape(2 * NZ, BLK, WIDE))
    grad_steer, grad_bias = reduce(
        q_latent, xq, latent_bias, xb, norm_gain, W.reshape(2, ql, QTWO), w_uk, pj, gl, gr
    )
    return (grad_steer, grad_bias)


def solution(mesh):
    in_specs = (
        P("ctx", None),
        P("ctx", None),
        P(),
        P("ctx", "head"),
        P("ctx", "head"),
        P("ctx", None),
        P("ctx", None),
        P(None, "head"),
        P(None, "head"),
        P("ctx", "head"),
        P(),
    )
    out_specs = (P("ctx", "head"), P("ctx", None))
    return jax.shard_map(shards, mesh=mesh, in_specs=in_specs, out_specs=out_specs, check_vma=False)
```

```python
import functools
import math

import jax
import jax.numpy as jnp
from jax import lax
from jax.experimental import pallas as pl
from jax.experimental.pallas import tpu as pltpu
from jax.sharding import PartitionSpec as P

KVL = 512
NOPE = 128
ROPE = 64
BLK = 128
WIDE = 640
HALF = 4
HEADW = NOPE + ROPE
QCOLS = HALF * HEADW
QTWO = QCOLS // 2
DCOLS = HALF * NOPE
EPS = 1e-06
LOWEST = -1e30
NZ = 16
NY = 4
MESH = pl.DeviceIdType.MESH
F32 = jnp.float32
BF16 = jnp.bfloat16
ANY = pl.BlockSpec(memory_space=pl.ANY)
HBM = pl.BlockSpec(memory_space=pltpu.HBM)
VM = pl.BlockSpec(memory_space=pltpu.VMEM)


def last_last(left, right):
    return lax.dot_general(left, right, (((1,), (1,)), ((), ())), preferred_element_type=F32)


def place():
    c = lax.axis_index("ctx")
    k = lax.axis_index("head")
    return c, k, c // NZ, lax.rem(c, NZ)


def gather_kernel(
    w_ref, q_ref, b_ref, s_ref, d_ref, kv_ref, kr_ref, uk_ref, uv_ref, gain_ref,
    W_out, KV_out, xq_out, xb_out, qg_out, qr_out, pj_out,
    qg, qr, pj, W, KV, own, rope, q2, bv, sv, dv, uk, uv, cq,
    w_s, w_r, z_s, z_r, y_s, y_r, f_s, f_r, x_s, x_r, c_s, c_r, m_s, m_r, loc, fill, drain,
):
    c, k, a, z = place()
    x_hi = k // 8
    y = lax.rem(k, 8) // 2
    core = lax.rem(k, 2)
    z_right = (a * NZ + lax.rem(z + 1, NZ), k)
    z_left = (a * NZ + lax.rem(z + NZ - 1, NZ), k)
    z_right2 = (a * NZ + lax.rem(z + 2, NZ), k)
    z_left2 = (a * NZ + lax.rem(z + NZ - 2, NZ), k)
    y_right = (c, x_hi * 8 + lax.rem(y + 1, NY) * 2 + core)
    y_left = (c, x_hi * 8 + lax.rem(y + NY - 1, NY) * 2 + core)
    sibling = (c, x_hi * 8 + y * 2 + (1 - core))
    pair = ((1 - a) * NZ + z, k)
    across = ((1 - a) * NZ + z, (1 - x_hi) * 8 + y * 2 + core)

    barrier = pltpu.get_barrier_semaphore()
    for dev in (z_right, z_left, z_right2, z_left2, y_right, y_left, sibling, pair, across):
        pl.semaphore_signal(barrier, inc=1, device_id=dev, device_id_type=MESH)

    my_d = pl.ds(pl.multiple_of(a * DCOLS, 128), DCOLS)
    fills = [
        pltpu.make_async_copy(q_ref, q2.at[0], fill.at[0]),
        pltpu.make_async_copy(b_ref, bv.at[0], fill.at[1]),
        pltpu.make_async_copy(s_ref, sv.at[0], fill.at[2]),
        pltpu.make_async_copy(d_ref.at[:, my_d], dv.at[0], fill.at[3]),
        pltpu.make_async_copy(uk_ref.at[:, my_d], uk, fill.at[4]),
        pltpu.make_async_copy(uv_ref.at[:, my_d], uv, fill.at[5]),
    ]
    load_k = pltpu.make_async_copy(kv_ref, own.at[:, pl.ds(0, KVL)], loc.at[2])
    load_r = pltpu.make_async_copy(kr_ref, rope, loc.at[3])
    load_k.start()
    load_r.start()
    load_r.wait()
    tall = jnp.concatenate([rope[...].astype(F32), jnp.zeros((WIDE - KVL - ROPE, BLK), F32)], axis=0)
    own[:, KVL:] = tall.T.astype(BF16)
    load_k.wait()
    for copy in fills:
        copy.start()
    pl.semaphore_wait(barrier, 9)

    sends = []

    def send(src, dst, s, r, dev):
        copy = pltpu.make_async_remote_copy(
            src_ref=src, dst_ref=dst, send_sem=s, recv_sem=r, device_id=dev, device_id_type=MESH
        )
        copy.start()
        sends.append(copy)

    def got(dst, s, r):
        pltpu.make_async_remote_copy(
            src_ref=dst, dst_ref=dst, send_sem=s, recv_sem=r, device_id=pair, device_id_type=MESH
        ).wait_recv()

    def columns(who, two):
        return pl.ds(pl.multiple_of(who * QCOLS + two * QTWO, 128), QTWO)

    their_d = pl.ds(pl.multiple_of((1 - a) * DCOLS, 128), DCOLS)

    counts = {(0, 0): 8, (0, 1): 7, (1, 0): 7, (1, 1): 8}

    def w_slot(part, two, zz):
        return W.at[two, (a if part == 0 else 1 - a) * NZ + lax.rem(zz + 2 * NZ, NZ)]

    def w_send(way, part, two, step):
        at = z - (step - 1) if way == 0 else z + (step - 1)
        slot = w_slot(part, two, at)
        src = w_ref.at[:, columns(a, two)] if step == 1 and part == 0 else slot
        n = 4 * way + 2 * part + two
        send(src, slot, w_s.at[n, step - 1], w_r.at[n, step - 1], z_left if way else z_right)

    def w(step):
        for part, two in ((0, 0), (0, 1), (1, 0), (1, 1)):
            for way in (0, 1):
                if step <= counts[way, part]:
                    n = 4 * way + 2 * part + two
                    at = z + step if way else z - step
                    got(w_slot(part, two, at), w_s.at[n, step - 1], w_r.at[n, step - 1])
                    if step + 1 <= counts[way, part]:
                        w_send(way, part, two, step + 1)

    rows = pl.ds(pl.multiple_of(core * 64 + y * 16, 16), 16)

    def far(way, step):
        return 0 if step == 0 else (2 * step if way else 2 * step - 1)

    def z_send(way, step):
        hop = 1 if step == 1 else 2
        src = own.at[rows] if step <= 2 else KV.at[a, far(way, step - 2), rows]
        dev = (z_left if way else z_right) if hop == 1 else (z_left2 if way else z_right2)
        send(src, KV.at[a, far(way, step), rows], z_s.at[way, step - 1], z_r.at[way, step - 1], dev)

    def kz(step):
        for way in range(2):
            if step <= 8 - way:
                got(KV.at[a, far(way, step), rows], z_s.at[way, step - 1], z_r.at[way, step - 1])
                if step + 2 <= 8 - way:
                    z_send(way, step + 2)

    def y_rows(shift):
        return pl.ds(pl.multiple_of(core * 64 + lax.rem(y + shift + NY, NY) * 16, 16), 16)

    def block(far_side, first, count, row):
        return KV.at[1 - a if far_side else a, pl.ds(first, count), row]

    def kx(q):
        for n, dev in ((0, pair), (1, across)):
            part = block(0, 4 * q + 2 * n, 2, rows)
            send(part, part, x_s.at[n, q], x_r.at[n, q], dev)

    def ky(q, far_side):
        if far_side:
            for n in range(2):
                got(block(1, 4 * q + 2 * n, 2, rows), x_s.at[n, q], x_r.at[n, q])
        part = block(far_side, 4 * q, 4, rows)
        for way in range(2):
            n = 2 * far_side + way
            send(part, part, y_s.at[n, q], y_r.at[n, q], y_left if way else y_right)

    def kf(q, far_side):
        for way in range(2):
            n = 2 * far_side + way
            row = y_rows(1 if way else -1)
            got(block(far_side, 4 * q, 4, row), y_s.at[n, q], y_r.at[n, q])
            part = block(far_side, 4 * q + 2 * way, 2, row)
            send(part, part, f_s.at[n, q], f_r.at[n, q], y_left if way else y_right)

    half = pl.ds(pl.multiple_of(core * 64, 16), 64)

    def kc(q):
        for far_side in range(2):
            for way in range(2):
                n = 2 * far_side + way
                got(block(far_side, 4 * q + 2 * way, 2, y_rows(2)), f_s.at[n, q], f_r.at[n, q])
        part = KV.at[:, pl.ds(4 * q, 4), half]
        send(part, part, c_s.at[q], c_r.at[q], sibling)

    for two in range(2):
        send(w_ref.at[:, columns(1 - a, two)], W.at[two, c], m_s.at[6 * two], m_r.at[6 * two], pair)
    for step in (1, 2):
        z_send(0, step)
        z_send(1, step)
    for two in range(2):
        w_send(0, 0, two, 1)
        w_send(1, 0, two, 1)
    copy_w = [pltpu.make_async_copy(w_ref.at[:, columns(a, two)], W.at[two, c], loc.at[4 * two]) for two in range(2)]
    for copy in copy_w:
        copy.start()
    copy_k = pltpu.make_async_copy(own.at[rows], KV.at[a, 0, rows], loc.at[1])
    copy_k.start()
    q_rows = pl.ds(pl.multiple_of(core * 64, 16), 64)
    send(q_ref.at[q_rows], q2.at[1, q_rows], m_s.at[1], m_r.at[1], pair)
    send(d_ref.at[:, their_d], dv.at[1], m_s.at[3], m_r.at[3], pair)
    send(b_ref, bv.at[1], m_s.at[4], m_r.at[4], pair)
    send(s_ref, sv.at[1], m_s.at[5], m_r.at[5], pair)
    for two in range(2):
        got(w_slot(1, two, z), m_s.at[6 * two], m_r.at[6 * two])
        w_send(0, 1, two, 1)
        w_send(1, 1, two, 1)

    both = 2 * BLK
    gain = gain_ref[...].reshape(1, gain_ref.shape[0])

    def norm(i):
        shifted = q2[i].astype(F32) + bv[i]
        inv = lax.rsqrt(jnp.mean(shifted * shifted, axis=1, keepdims=True) + EPS)
        cq[i] = (shifted * inv * gain).astype(BF16)

    def absorb_g(i):
        for h in range(HALF):
            up = slice(h * NOPE, (h + 1) * NOPE)
            qg[i, (HALF + h) * BLK : (HALF + h + 1) * BLK, :] = last_last(dv[i, :, up], uv[:, up]).astype(BF16)

    other = pl.ds(pl.multiple_of((1 - core) * 64, 16), 64)
    drains = []

    def store(src, dst):
        drains.append(pltpu.make_async_copy(src, dst, drain.at[len(drains)]))
        drains[-1].start()

    def kend(q):
        got(KV.at[:, pl.ds(4 * q, 4), other], c_s.at[q], c_r.at[q])
        store(KV.at[:, pl.ds(4 * q, 4)], KV_out.at[:, pl.ds(4 * q, 4)])

    for copy in fills:
        copy.wait()
    norm(0)
    kz(1)
    kz(2)
    copy_k.wait()
    kx(0)
    ky(0, 0)
    w(1)
    kz(3)
    ky(0, 1)
    kz(4)
    kx(1)
    ky(1, 0)
    w(2)
    kf(0, 0)
    kz(5)
    ky(1, 1)
    kz(6)
    kx(2)
    ky(2, 0)
    w(3)
    kf(0, 1)
    kf(1, 0)
    got(q2.at[1, q_rows], m_s.at[1], m_r.at[1])
    send(q2.at[1, q_rows], q2.at[1, q_rows], m_s.at[2], m_r.at[2], sibling)
    kz(7)
    ky(2, 1)
    kz(8)
    kx(3)
    ky(3, 0)
    w(4)
    absorb_g(0)
    kf(1, 1)
    ky(3, 1)
    w(5)
    kf(2, 0)
    kc(0)
    got(q2.at[1, other], m_s.at[2], m_r.at[2])
    got(dv.at[1], m_s.at[3], m_r.at[3])
    got(bv.at[1], m_s.at[4], m_r.at[4])
    got(sv.at[1], m_s.at[5], m_r.at[5])
    store(q2.at[1], xq_out)
    store(bv.at[1], xb_out)
    norm(1)
    w(6)
    kf(2, 1)
    kf(3, 0)
    kc(1)
    kend(0)
    absorb_g(1)
    store(qg.at[:, pl.ds(HALF * BLK, HALF * BLK)], qg_out.at[:, pl.ds(HALF * BLK, HALF * BLK)])
    w(7)
    kf(3, 1)
    kc(2)
    kend(1)
    w(8)
    kc(3)
    for copy in copy_w:
        copy.wait()
    store(W, W_out)
    c_query = cq[...].reshape(both, cq.shape[2])
    for two in range(2):
        weights = W[two].reshape(cq.shape[2], QTWO)
        proj = jnp.dot(c_query, weights, preferred_element_type=F32)
        pj[two] = proj
        store(pj.at[two], pj_out.at[two])
        query = []
        for i in range(2):
            row = sv[i]
            part = slice(two * QTWO, (two + 1) * QTWO)
            rest = slice(QCOLS + two * QTWO, QCOLS + (two + 1) * QTWO)
            query.append(proj[i * BLK : (i + 1) * BLK] + jnp.where(a == 0, row[:, part], row[:, rest]))
        query = jnp.concatenate(query, axis=0).astype(BF16)
        for local in range(2):
            h = 2 * two + local
            at = local * HEADW
            q = last_last(query[:, at : at + NOPE], uk[:, h * NOPE : (h + 1) * NOPE]).astype(BF16)
            pos = query[:, at + NOPE : at + HEADW]
            pos = jnp.concatenate([pos, jnp.zeros((both, WIDE - KVL - ROPE), BF16)], axis=1)
            for i in range(2):
                qg[i, h * BLK : (h + 1) * BLK, :] = q[i * BLK : (i + 1) * BLK]
                qr[i, h * BLK : (h + 1) * BLK, :] = pos[i * BLK : (i + 1) * BLK]
        done = pl.ds(2 * two * BLK, 2 * BLK)
        store(qg.at[:, done], qg_out.at[:, done])
    store(qr, qr_out)
    kend(2)
    kend(3)
    for copy in drains:
        copy.wait()
    for copy in sends:
        copy.wait_send()


def gather(w_q, q_latent, latent_bias, steer, d_out, kv_latent, key_rope, w_uk, w_uv, gain):
    def dma(*shape):
        return pltpu.SemaphoreType.DMA(shape)

    ql = q_latent.shape[1]
    rows = HALF * BLK
    w_shape = (2, 2 * NZ, w_q.shape[0], QTWO)
    k_shape = (2, NZ, BLK, WIDE)
    return pl.pallas_call(
        gather_kernel,
        out_shape=(
            jax.ShapeDtypeStruct(w_shape, BF16),
            jax.ShapeDtypeStruct(k_shape, BF16),
            jax.ShapeDtypeStruct(q_latent.shape, BF16),
            jax.ShapeDtypeStruct(latent_bias.shape, F32),
            jax.ShapeDtypeStruct((2, 2 * rows, KVL), BF16),
            jax.ShapeDtypeStruct((2, rows, WIDE - KVL), BF16),
            jax.ShapeDtypeStruct((2, 2 * BLK, QTWO), F32),
        ),
        in_specs=[HBM] * 9 + [VM],
        out_specs=[HBM] * 7,
        scratch_shapes=[
            pltpu.VMEM((2, 2 * rows, KVL), BF16),
            pltpu.VMEM((2, rows, WIDE - KVL), BF16),
            pltpu.VMEM((2, 2 * BLK, QTWO), F32),
            pltpu.VMEM(w_shape, BF16),
            pltpu.VMEM(k_shape, BF16),
            pltpu.VMEM((BLK, WIDE), BF16),
            pltpu.VMEM((ROPE, BLK), BF16),
            pltpu.VMEM((2, BLK, ql), BF16),
            pltpu.VMEM((2, 1, ql), F32),
            pltpu.VMEM((2, 1, 2 * QCOLS), F32),
            pltpu.VMEM((2, BLK, DCOLS), BF16),
            pltpu.VMEM((KVL, DCOLS), BF16),
            pltpu.VMEM((KVL, DCOLS), BF16),
            pltpu.VMEM((2, BLK, ql), BF16),
            dma(8, 8), dma(8, 8), dma(2, 8), dma(2, 8), dma(4, 4), dma(4, 4), dma(4, 4), dma(4, 4),
            dma(2, 4), dma(2, 4), dma(4), dma(4), dma(7), dma(7), dma(5), dma(6), dma(16),
        ],
        compiler_params=pltpu.CompilerParams(
            collective_id=0, has_side_effects=True, vmem_limit_bytes=54 * 2**20
        ),
        cost_estimate=pl.CostEstimate(flops=2_000_000_000, bytes_accessed=20_000_000, transcendentals=0),
        name="gather",
    )(w_q, q_latent, latent_bias, steer, d_out, kv_latent, key_rope, w_uk, w_uv, gain)


CHUNK = 256
TILES = CHUNK // BLK


def attend_kernel(
    mask, qg_ref, qr_ref, KV, gl, gr, keys_all, qg, qr, sbuf, dbuf, acc, peak, lsum, gsum, index, sem
):
    c, k, a, z = place()
    scale = HEADW ** (-0.5)
    scale2 = scale * math.log2(math.e)
    rows = HALF * BLK
    loads = [
        pltpu.make_async_copy(qg_ref.at[0], qg.at[0], sem.at[0]),
        pltpu.make_async_copy(qr_ref, qr, sem.at[1]),
        pltpu.make_async_copy(KV, keys_all, sem.at[2]),
        pltpu.make_async_copy(qg_ref.at[1], qg.at[1], sem.at[3]),
    ]
    for copy in loads:
        copy.start()

    live = []
    for i in range(2):
        block = c if i == 0 else lax.rem(c + NZ, 2 * NZ)

        def visit(j, n):
            far = lax.rem(z - lax.rem(j, NZ) + NZ, NZ)
            slot = jnp.where(far == 0, 0, jnp.where(far <= NZ // 2, 2 * far - 1, 2 * (NZ - far)))
            index[i, n] = (j // NZ) * NZ + slot
            return n + jnp.where(mask[block, j] > 0, 1, 0)

        n = lax.fori_loop(0, 2 * NZ, visit, 0)
        for extra in range(TILES - 1):
            index[i, n + extra] = 0
        live.append(n)

    def chunks_of(n):
        return (n + TILES - 1) // TILES

    def keys_of(i, t):
        return jnp.concatenate([keys_all[index[i, t * TILES + d]] for d in range(TILES)], axis=0)

    def in_fours(count, step):
        def four(t, _):
            step(4 * t, 4)
            return 0

        lax.fori_loop(0, count // 4, four, 0)
        rest = lax.rem(count, 4)

        @pl.when(rest >= 2)
        def _():
            step(count - rest, 2)

        @pl.when(lax.rem(rest, 2) == 1)
        def _():
            step(count - 1, 1)

    def in_pairs(count, step):
        def pair(t, _):
            step(2 * t, 2)
            return 0

        lax.fori_loop(0, count // 2, pair, 0)

        @pl.when(lax.rem(count, 2) == 1)
        def _():
            step(count - 1, 1)

    for i in range(2):
        n = live[i]
        count = chunks_of(n)

        for copy in loads[3 * i : 3 * i + 3]:
            copy.wait()
        peak[...] = jnp.full((rows, 128), LOWEST, F32)
        lsum[...] = jnp.zeros((rows, 128), F32)
        gsum[...] = jnp.zeros((rows, 128), F32)
        acc[...] = jnp.zeros((rows, WIDE), F32)

        def scores(first, many):
            top = peak[...]
            for t in [first + d for d in range(many)]:
                keys = keys_of(i, t)
                column = lax.broadcasted_iota(jnp.int32, (1, CHUNK), 1) + t * CHUNK
                dead = jnp.where(column < n * BLK, 0.0, LOWEST)
                main = last_last(qg[i], keys[:, :KVL])
                s = main[:rows] + last_last(qr[i], keys[:, KVL:]) + dead
                sbuf[t] = s
                dbuf[t] = main[rows:]
                for part in range(TILES):
                    top = jnp.maximum(top, s[:, part * 128 : (part + 1) * 128])
            peak[...] = top

        in_pairs(count, scores)
        top = jnp.max(peak[...], axis=1, keepdims=True) * scale2

        def weigh(first, many):
            low = lsum[...]
            gow = gsum[...]
            for t in [first + d for d in range(many)]:
                e = jnp.exp2(sbuf[t] * scale2 - top)
                sbuf[t] = e
                mixed = e * dbuf[t]
                low = low + sum(e[:, p * 128 : (p + 1) * 128] for p in range(TILES))
                gow = gow + sum(mixed[:, p * 128 : (p + 1) * 128] for p in range(TILES))
            lsum[...] = low
            gsum[...] = gow

        in_pairs(count, weigh)
        total = jnp.sum(lsum[...], axis=1, keepdims=True)
        ratio = jnp.sum(gsum[...], axis=1, keepdims=True) / total

        def collect(first, many):
            weight = jnp.concatenate(
                [(sbuf[first + d] * (dbuf[first + d] - ratio)).astype(BF16) for d in range(many)], axis=1
            )
            keys = jnp.concatenate([keys_of(i, first + d) for d in range(many)], axis=0)
            acc[...] += jnp.dot(weight, keys, preferred_element_type=F32)

        in_fours(count, collect)
        grad = acc[...] * (scale / total)
        gl[i] = grad[:, :KVL].astype(BF16).reshape(HALF, BLK, KVL)
        gr[i] = grad[:, KVL:].reshape(HALF, BLK, WIDE - KVL)


def attend(mask, qg, qr, KV):
    rows = HALF * BLK
    nchunk = 2 * NZ // TILES
    return pl.pallas_call(
        attend_kernel,
        out_shape=(
            jax.ShapeDtypeStruct((2, HALF, BLK, KVL), BF16),
            jax.ShapeDtypeStruct((2, HALF, BLK, WIDE - KVL), F32),
        ),
        in_specs=[pl.BlockSpec(memory_space=pltpu.SMEM), HBM, HBM, HBM],
        out_specs=[VM, VM],
        scratch_shapes=[
            pltpu.VMEM((2 * NZ, BLK, WIDE), BF16),
            pltpu.VMEM((2, 2 * rows, KVL), BF16),
            pltpu.VMEM((2, rows, WIDE - KVL), BF16),
            pltpu.VMEM((nchunk, rows, CHUNK), F32),
            pltpu.VMEM((nchunk, rows, CHUNK), F32),
            pltpu.VMEM((rows, WIDE), F32),
            pltpu.VMEM((rows, 128), F32),
            pltpu.VMEM((rows, 128), F32),
            pltpu.VMEM((rows, 128), F32),
            pltpu.SMEM((2, 2 * NZ + TILES), jnp.int32),
            pltpu.SemaphoreType.DMA((4,)),
        ],
        compiler_params=pltpu.CompilerParams(vmem_limit_bytes=54 * 2**20),
        cost_estimate=pl.CostEstimate(flops=10_000_000_000, bytes_accessed=10_000_000, transcendentals=4_000_000),
        name="attend",
    )(mask, qg, qr, KV)


def reduce_kernel(
    q_ref, xq_ref, b_ref, xb_ref, gain_ref, W_ref, uk_ref, pj_ref, gl_ref, gr_ref,
    steer_out, bias_out,
    q2, Wv, uk, pj, gl, gr, u_ref, gs_ref, lb_ref, rbuf, rgs, p_s, p_r, g_s, g_r, sem,
):
    c, k, a, z = place()
    pair_c = (1 - a) * NZ + z
    n = 16

    def mate(side, shift):
        return (pair_c if side else c, lax.rem(k + shift, n))

    my_d = pl.ds(pl.multiple_of(a * DCOLS, 128), DCOLS)
    loads = [
        pltpu.make_async_copy(gl_ref, gl, sem.at[0]),
        pltpu.make_async_copy(uk_ref.at[:, my_d], uk, sem.at[1]),
        pltpu.make_async_copy(gr_ref, gr, sem.at[2]),
        pltpu.make_async_copy(pj_ref, pj, sem.at[3]),
        pltpu.make_async_copy(q_ref, q2.at[0], sem.at[4]),
        pltpu.make_async_copy(xq_ref, q2.at[1], sem.at[5]),
        pltpu.make_async_copy(W_ref, Wv, sem.at[6]),
    ]
    for load in loads:
        load.start()
    others = [(side, shift) for side in range(2) for shift in range(n) if side or shift]
    barrier = pltpu.get_barrier_semaphore()
    for one in others:
        pl.semaphore_signal(barrier, inc=1, device_id=mate(*one), device_id_type=MESH)
    both = 2 * BLK
    gain = gain_ref[...].reshape(1, gain_ref.shape[0])
    for load in loads:
        load.wait()
    pieces = []
    for h in range(HALF):
        pieces.append(
            jnp.dot(gl[:, h].reshape(both, KVL), uk[:, h * NOPE : (h + 1) * NOPE], preferred_element_type=F32)
        )
        pieces.append(gr[:, h].reshape(both, WIDE - KVL)[:, :ROPE])
    all_grads = jnp.concatenate(pieces, axis=1)
    u_ref[...] = jnp.zeros_like(u_ref)
    for i in range(2):
        shifted = q2[i].astype(F32) + (b_ref, xb_ref)[i][...]
        inv = lax.rsqrt(jnp.mean(shifted * shifted, axis=1, keepdims=True) + EPS)
        grad_query = all_grads[i * BLK : (i + 1) * BLK]
        gs_ref[i : i + 1, :] = jnp.sum(grad_query, axis=0, keepdims=True)
        lean = sum(
            jnp.sum(
                grad_query[:, two * QTWO : (two + 1) * QTWO] * pj[two, i * BLK : (i + 1) * BLK, :], axis=1, keepdims=True
            )
            for two in range(2)
        )
        u = jnp.sum(grad_query * inv, axis=0, keepdims=True)
        u_high = u.astype(BF16)
        u_ref[2 * i : 2 * i + 1, :] = u_high.astype(F32)
        u_ref[2 * i + 1 : 2 * i + 2, :] = u - u_high.astype(F32)
        lb_ref[i : i + 1, :] = jnp.sum(shifted * (inv * inv * lean), axis=0, keepdims=True)

    back = sum(
        last_last(u_ref[:, two * QTWO : (two + 1) * QTWO].astype(BF16), Wv[two]) for two in range(2)
    )
    for i in range(2):
        whole = back[2 * i : 2 * i + 1] + back[2 * i + 1 : 2 * i + 2]
        lb_ref[i : i + 1, :] = gain * whole - lb_ref[i : i + 1, :] * (1.0 / gain.shape[1])
    pl.semaphore_wait(barrier, len(others))

    def copy(src, dst, s, r, dev):
        return pltpu.make_async_remote_copy(
            src_ref=src, dst_ref=dst, send_sem=s, recv_sem=r, device_id=dev, device_id_type=MESH
        )

    steer_copy = copy(gs_ref.at[pl.ds(1, 1)], rgs, p_s.at[0], p_r.at[0], mate(1, 0))
    steer_copy.start()
    out = []
    for side, shift in others:
        at = side * n + shift
        out.append(
            copy(lb_ref.at[pl.ds(side, 1)], rbuf.at[at], g_s.at[at], g_r.at[at], mate(side, shift))
        )
        out[-1].start()
    steer_copy.wait_recv()
    mine = gs_ref[0:1, :]
    theirs = rgs[...]
    steer_out[:, :QCOLS] = jnp.where(a == 0, mine, theirs)
    steer_out[:, QCOLS:] = jnp.where(a == 0, theirs, mine)
    result = lb_ref[0:1, :]
    for (side, shift), one in zip(others, out):
        one.wait_recv()
        result = result + rbuf[side * n + shift]
    bias_out[...] = result
    steer_copy.wait_send()
    for one in out:
        one.wait_send()


def reduce(q, xq, b, xb, gain, W, w_uk, pj, gl, gr):
    ql = q.shape[1]
    return pl.pallas_call(
        reduce_kernel,
        out_shape=(jax.ShapeDtypeStruct((1, 2 * QCOLS), F32), jax.ShapeDtypeStruct((1, ql), F32)),
        in_specs=[HBM, HBM, VM, VM, VM, HBM, HBM, HBM, HBM, HBM],
        out_specs=[VM, VM],
        scratch_shapes=[
            pltpu.VMEM((2, BLK, ql), BF16),
            pltpu.VMEM((2, ql, QTWO), BF16),
            pltpu.VMEM((KVL, DCOLS), BF16),
            pltpu.VMEM((2, 2 * BLK, QTWO), F32),
            pltpu.VMEM((2, HALF, BLK, KVL), BF16),
            pltpu.VMEM((2, HALF, BLK, WIDE - KVL), F32),
            pltpu.VMEM((16, QCOLS), F32),
            pltpu.VMEM((2, QCOLS), F32),
            pltpu.VMEM((2, ql), F32),
            pltpu.VMEM((32, 1, ql), F32),
            pltpu.VMEM((1, QCOLS), F32),
            pltpu.SemaphoreType.DMA((1,)),
            pltpu.SemaphoreType.DMA((1,)),
            pltpu.SemaphoreType.DMA((32,)),
            pltpu.SemaphoreType.DMA((32,)),
            pltpu.SemaphoreType.DMA((7,)),
        ],
        compiler_params=pltpu.CompilerParams(
            collective_id=1, has_side_effects=True, vmem_limit_bytes=54 * 2**20
        ),
        name="reduce",
    )(q, xq, b, xb, gain, W, w_uk, pj, gl, gr)


def shards(
    q_latent, latent_bias, norm_gain, w_q, steer, kv_latent, key_rope, w_uk, w_uv, d_out, block_mask
):
    ql = q_latent.shape[1]
    W, KV, xq, xb, qg, qr, pj = gather(
        w_q, q_latent, latent_bias, steer, d_out, kv_latent, key_rope.T, w_uk, w_uv, norm_gain
    )
    gl, gr = attend(block_mask, qg, qr, KV.reshape(2 * NZ, BLK, WIDE))
    grad_steer, grad_bias = reduce(
        q_latent, xq, latent_bias, xb, norm_gain, W.reshape(2, ql, QTWO), w_uk, pj, gl, gr
    )
    return (grad_steer, grad_bias)


def solution(mesh):
    in_specs = (
        P("ctx", None),
        P("ctx", None),
        P(),
        P("ctx", "head"),
        P("ctx", "head"),
        P("ctx", None),
        P("ctx", None),
        P(None, "head"),
        P(None, "head"),
        P("ctx", "head"),
        P(),
    )
    out_specs = (P("ctx", "head"), P("ctx", None))
    return jax.shard_map(shards, mesh=mesh, in_specs=in_specs, out_specs=out_specs, check_vma=False)
```

```python
import functools
import math

import jax
import jax.numpy as jnp
from jax import lax
from jax.experimental import pallas as pl
from jax.experimental.pallas import tpu as pltpu
from jax.sharding import PartitionSpec as P

KVL = 512
NOPE = 128
ROPE = 64
BLK = 128
WIDE = 640
HALF = 4
HEADW = NOPE + ROPE
QCOLS = HALF * HEADW
QTWO = QCOLS // 2
DCOLS = HALF * NOPE
EPS = 1e-06
LOWEST = -1e30
NZ = 16
NY = 4
MESH = pl.DeviceIdType.MESH
F32 = jnp.float32
BF16 = jnp.bfloat16
ANY = pl.BlockSpec(memory_space=pl.ANY)
HBM = pl.BlockSpec(memory_space=pltpu.HBM)
VM = pl.BlockSpec(memory_space=pltpu.VMEM)


def last_last(left, right):
    return lax.dot_general(left, right, (((1,), (1,)), ((), ())), preferred_element_type=F32)


def place():
    c = lax.axis_index("ctx")
    k = lax.axis_index("head")
    return c, k, c // NZ, lax.rem(c, NZ)


def gather_kernel(
    w_ref, q_ref, b_ref, s_ref, d_ref, kv_ref, kr_ref, uk_ref, uv_ref, gain_ref,
    W_out, KV_out, xq_out, xb_out, qg_out, qr_out, pj_out,
    qg, qr, pj, W, KV, own, rope, q2, bv, sv, dv, uk, uv, cq,
    w_s, w_r, z_s, z_r, y_s, y_r, f_s, f_r, x_s, x_r, c_s, c_r, m_s, m_r, loc, fill, drain,
):
    c, k, a, z = place()
    x_hi = k // 8
    y = lax.rem(k, 8) // 2
    core = lax.rem(k, 2)
    z_right = (a * NZ + lax.rem(z + 1, NZ), k)
    z_left = (a * NZ + lax.rem(z + NZ - 1, NZ), k)
    z_right2 = (a * NZ + lax.rem(z + 2, NZ), k)
    z_left2 = (a * NZ + lax.rem(z + NZ - 2, NZ), k)
    y_right = (c, x_hi * 8 + lax.rem(y + 1, NY) * 2 + core)
    y_left = (c, x_hi * 8 + lax.rem(y + NY - 1, NY) * 2 + core)
    sibling = (c, x_hi * 8 + y * 2 + (1 - core))
    pair = ((1 - a) * NZ + z, k)
    across = ((1 - a) * NZ + z, (1 - x_hi) * 8 + y * 2 + core)

    barrier = pltpu.get_barrier_semaphore()
    for dev in (z_right, z_left, z_right2, z_left2, y_right, y_left, sibling, pair, across):
        pl.semaphore_signal(barrier, inc=1, device_id=dev, device_id_type=MESH)

    my_d = pl.ds(pl.multiple_of(a * DCOLS, 128), DCOLS)
    fills = [
        pltpu.make_async_copy(q_ref, q2.at[0], fill.at[0]),
        pltpu.make_async_copy(b_ref, bv.at[0], fill.at[1]),
        pltpu.make_async_copy(s_ref, sv.at[0], fill.at[2]),
        pltpu.make_async_copy(d_ref.at[:, my_d], dv.at[0], fill.at[3]),
        pltpu.make_async_copy(uk_ref.at[:, my_d], uk, fill.at[4]),
        pltpu.make_async_copy(uv_ref.at[:, my_d], uv, fill.at[5]),
    ]
    load_k = pltpu.make_async_copy(kv_ref, own.at[:, pl.ds(0, KVL)], loc.at[2])
    load_r = pltpu.make_async_copy(kr_ref, rope, loc.at[3])
    load_k.start()
    load_r.start()
    load_r.wait()
    tall = jnp.concatenate([rope[...].astype(F32), jnp.zeros((WIDE - KVL - ROPE, BLK), F32)], axis=0)
    own[:, KVL:] = tall.T.astype(BF16)
    load_k.wait()
    for copy in fills:
        copy.start()
    pl.semaphore_wait(barrier, 9)

    sends = []

    def send(src, dst, s, r, dev):
        copy = pltpu.make_async_remote_copy(
            src_ref=src, dst_ref=dst, send_sem=s, recv_sem=r, device_id=dev, device_id_type=MESH
        )
        copy.start()
        sends.append(copy)

    def got(dst, s, r):
        pltpu.make_async_remote_copy(
            src_ref=dst, dst_ref=dst, send_sem=s, recv_sem=r, device_id=pair, device_id_type=MESH
        ).wait_recv()

    def columns(who, two):
        return pl.ds(pl.multiple_of(who * QCOLS + two * QTWO, 128), QTWO)

    their_d = pl.ds(pl.multiple_of((1 - a) * DCOLS, 128), DCOLS)

    counts = {(0, 0): 8, (0, 1): 7, (1, 0): 7, (1, 1): 8}

    def w_slot(part, two, zz):
        return W.at[two, (a if part == 0 else 1 - a) * NZ + lax.rem(zz + 2 * NZ, NZ)]

    def w_send(way, part, two, step):
        at = z - (step - 1) if way == 0 else z + (step - 1)
        slot = w_slot(part, two, at)
        src = w_ref.at[:, columns(a, two)] if step == 1 and part == 0 else slot
        n = 4 * way + 2 * part + two
        send(src, slot, w_s.at[n, step - 1], w_r.at[n, step - 1], z_left if way else z_right)

    def w(step):
        for part, two in ((0, 0), (0, 1), (1, 0), (1, 1)):
            for way in (0, 1):
                if step <= counts[way, part]:
                    n = 4 * way + 2 * part + two
                    at = z + step if way else z - step
                    got(w_slot(part, two, at), w_s.at[n, step - 1], w_r.at[n, step - 1])
                    if step + 1 <= counts[way, part]:
                        w_send(way, part, two, step + 1)

    rows = pl.ds(pl.multiple_of(core * 64 + y * 16, 16), 16)

    def far(way, step):
        return 0 if step == 0 else (2 * step if way else 2 * step - 1)

    def z_send(way, step):
        hop = 1 if step == 1 else 2
        src = own.at[rows] if step <= 2 else KV.at[a, far(way, step - 2), rows]
        dev = (z_left if way else z_right) if hop == 1 else (z_left2 if way else z_right2)
        send(src, KV.at[a, far(way, step), rows], z_s.at[way, step - 1], z_r.at[way, step - 1], dev)

    def kz(step):
        for way in range(2):
            if step <= 8 - way:
                got(KV.at[a, far(way, step), rows], z_s.at[way, step - 1], z_r.at[way, step - 1])
                if step + 2 <= 8 - way:
                    z_send(way, step + 2)

    def y_rows(shift):
        return pl.ds(pl.multiple_of(core * 64 + lax.rem(y + shift + NY, NY) * 16, 16), 16)

    def block(far_side, first, count, row):
        return KV.at[1 - a if far_side else a, pl.ds(first, count), row]

    def kx(q):
        for n, dev in ((0, pair), (1, across)):
            part = block(0, 4 * q + 2 * n, 2, rows)
            send(part, part, x_s.at[n, q], x_r.at[n, q], dev)

    def ky(q, far_side):
        if far_side:
            for n in range(2):
                got(block(1, 4 * q + 2 * n, 2, rows), x_s.at[n, q], x_r.at[n, q])
        part = block(far_side, 4 * q, 4, rows)
        for way in range(2):
            n = 2 * far_side + way
            send(part, part, y_s.at[n, q], y_r.at[n, q], y_left if way else y_right)

    def kf(q, far_side):
        for way in range(2):
            n = 2 * far_side + way
            row = y_rows(1 if way else -1)
            got(block(far_side, 4 * q, 4, row), y_s.at[n, q], y_r.at[n, q])
            part = block(far_side, 4 * q + 2 * way, 2, row)
            send(part, part, f_s.at[n, q], f_r.at[n, q], y_left if way else y_right)

    half = pl.ds(pl.multiple_of(core * 64, 16), 64)

    def kc(q):
        for far_side in range(2):
            for way in range(2):
                n = 2 * far_side + way
                got(block(far_side, 4 * q + 2 * way, 2, y_rows(2)), f_s.at[n, q], f_r.at[n, q])
        part = KV.at[:, pl.ds(4 * q, 4), half]
        send(part, part, c_s.at[q], c_r.at[q], sibling)

    for two in range(2):
        send(w_ref.at[:, columns(1 - a, two)], W.at[two, c], m_s.at[6 * two], m_r.at[6 * two], pair)
    for step in (1, 2):
        z_send(0, step)
        z_send(1, step)
    for two in range(2):
        w_send(0, 0, two, 1)
        w_send(1, 0, two, 1)
    copy_w = [pltpu.make_async_copy(w_ref.at[:, columns(a, two)], W.at[two, c], loc.at[4 * two]) for two in range(2)]
    for copy in copy_w:
        copy.start()
    copy_k = pltpu.make_async_copy(own.at[rows], KV.at[a, 0, rows], loc.at[1])
    copy_k.start()
    q_rows = pl.ds(pl.multiple_of(core * 64, 16), 64)
    send(q_ref.at[q_rows], q2.at[1, q_rows], m_s.at[1], m_r.at[1], pair)
    send(d_ref.at[:, their_d], dv.at[1], m_s.at[3], m_r.at[3], pair)
    send(b_ref, bv.at[1], m_s.at[4], m_r.at[4], pair)
    send(s_ref, sv.at[1], m_s.at[5], m_r.at[5], pair)
    for two in range(2):
        got(w_slot(1, two, z), m_s.at[6 * two], m_r.at[6 * two])
        w_send(0, 1, two, 1)
        w_send(1, 1, two, 1)

    both = 2 * BLK
    gain = gain_ref[...].reshape(1, gain_ref.shape[0])

    def norm(i):
        shifted = q2[i].astype(F32) + bv[i]
        inv = lax.rsqrt(jnp.mean(shifted * shifted, axis=1, keepdims=True) + EPS)
        cq[i] = (shifted * inv * gain).astype(BF16)

    def absorb_g(i):
        for h in range(HALF):
            up = slice(h * NOPE, (h + 1) * NOPE)
            qg[i, (HALF + h) * BLK : (HALF + h + 1) * BLK, :] = last_last(dv[i, :, up], uv[:, up]).astype(BF16)

    other = pl.ds(pl.multiple_of((1 - core) * 64, 16), 64)
    drains = []

    def store(src, dst):
        drains.append(pltpu.make_async_copy(src, dst, drain.at[len(drains)]))
        drains[-1].start()

    def kend(q):
        got(KV.at[:, pl.ds(4 * q, 4), other], c_s.at[q], c_r.at[q])
        store(KV.at[:, pl.ds(4 * q, 4)], KV_out.at[:, pl.ds(4 * q, 4)])

    for copy in fills:
        copy.wait()
    norm(0)
    kz(1)
    kz(2)
    copy_k.wait()
    kx(0)
    ky(0, 0)
    w(1)
    kz(3)
    ky(0, 1)
    kz(4)
    kx(1)
    ky(1, 0)
    w(2)
    kf(0, 0)
    kz(5)
    ky(1, 1)
    kz(6)
    kx(2)
    ky(2, 0)
    w(3)
    kf(0, 1)
    kf(1, 0)
    got(q2.at[1, q_rows], m_s.at[1], m_r.at[1])
    send(q2.at[1, q_rows], q2.at[1, q_rows], m_s.at[2], m_r.at[2], sibling)
    kz(7)
    ky(2, 1)
    kz(8)
    kx(3)
    ky(3, 0)
    w(4)
    absorb_g(0)
    kf(1, 1)
    ky(3, 1)
    w(5)
    kf(2, 0)
    kc(0)
    got(q2.at[1, other], m_s.at[2], m_r.at[2])
    got(dv.at[1], m_s.at[3], m_r.at[3])
    got(bv.at[1], m_s.at[4], m_r.at[4])
    got(sv.at[1], m_s.at[5], m_r.at[5])
    store(q2.at[1], xq_out)
    store(bv.at[1], xb_out)
    norm(1)
    w(6)
    kf(2, 1)
    kf(3, 0)
    kc(1)
    kend(0)
    absorb_g(1)
    store(qg.at[:, pl.ds(HALF * BLK, HALF * BLK)], qg_out.at[:, pl.ds(HALF * BLK, HALF * BLK)])
    w(7)
    kf(3, 1)
    kc(2)
    kend(1)
    w(8)
    kc(3)
    for copy in copy_w:
        copy.wait()
    store(W, W_out)
    c_query = cq[...].reshape(both, cq.shape[2])
    for two in range(2):
        weights = W[two].reshape(cq.shape[2], QTWO)
        proj = jnp.dot(c_query, weights, preferred_element_type=F32)
        pj[two] = proj
        store(pj.at[two], pj_out.at[two])
        query = []
        for i in range(2):
            row = sv[i]
            part = slice(two * QTWO, (two + 1) * QTWO)
            rest = slice(QCOLS + two * QTWO, QCOLS + (two + 1) * QTWO)
            query.append(proj[i * BLK : (i + 1) * BLK] + jnp.where(a == 0, row[:, part], row[:, rest]))
        query = jnp.concatenate(query, axis=0).astype(BF16)
        for local in range(2):
            h = 2 * two + local
            at = local * HEADW
            q = last_last(query[:, at : at + NOPE], uk[:, h * NOPE : (h + 1) * NOPE]).astype(BF16)
            pos = query[:, at + NOPE : at + HEADW]
            pos = jnp.concatenate([pos, jnp.zeros((both, WIDE - KVL - ROPE), BF16)], axis=1)
            for i in range(2):
                qg[i, h * BLK : (h + 1) * BLK, :] = q[i * BLK : (i + 1) * BLK]
                qr[i, h * BLK : (h + 1) * BLK, :] = pos[i * BLK : (i + 1) * BLK]
        done = pl.ds(2 * two * BLK, 2 * BLK)
        store(qg.at[:, done], qg_out.at[:, done])
    store(qr, qr_out)
    kend(2)
    kend(3)
    for copy in drains:
        copy.wait()
    for copy in sends:
        copy.wait_send()


def gather(w_q, q_latent, latent_bias, steer, d_out, kv_latent, key_rope, w_uk, w_uv, gain):
    def dma(*shape):
        return pltpu.SemaphoreType.DMA(shape)

    ql = q_latent.shape[1]
    rows = HALF * BLK
    w_shape = (2, 2 * NZ, w_q.shape[0], QTWO)
    k_shape = (2, NZ, BLK, WIDE)
    return pl.pallas_call(
        gather_kernel,
        out_shape=(
            jax.ShapeDtypeStruct(w_shape, BF16),
            jax.ShapeDtypeStruct(k_shape, BF16),
            jax.ShapeDtypeStruct(q_latent.shape, BF16),
            jax.ShapeDtypeStruct(latent_bias.shape, F32),
            jax.ShapeDtypeStruct((2, 2 * rows, KVL), BF16),
            jax.ShapeDtypeStruct((2, rows, WIDE - KVL), BF16),
            jax.ShapeDtypeStruct((2, 2 * BLK, QTWO), F32),
        ),
        in_specs=[HBM] * 9 + [VM],
        out_specs=[HBM] * 7,
        scratch_shapes=[
            pltpu.VMEM((2, 2 * rows, KVL), BF16),
            pltpu.VMEM((2, rows, WIDE - KVL), BF16),
            pltpu.VMEM((2, 2 * BLK, QTWO), F32),
            pltpu.VMEM(w_shape, BF16),
            pltpu.VMEM(k_shape, BF16),
            pltpu.VMEM((BLK, WIDE), BF16),
            pltpu.VMEM((ROPE, BLK), BF16),
            pltpu.VMEM((2, BLK, ql), BF16),
            pltpu.VMEM((2, 1, ql), F32),
            pltpu.VMEM((2, 1, 2 * QCOLS), F32),
            pltpu.VMEM((2, BLK, DCOLS), BF16),
            pltpu.VMEM((KVL, DCOLS), BF16),
            pltpu.VMEM((KVL, DCOLS), BF16),
            pltpu.VMEM((2, BLK, ql), BF16),
            dma(8, 8), dma(8, 8), dma(2, 8), dma(2, 8), dma(4, 4), dma(4, 4), dma(4, 4), dma(4, 4),
            dma(2, 4), dma(2, 4), dma(4), dma(4), dma(7), dma(7), dma(5), dma(6), dma(16),
        ],
        compiler_params=pltpu.CompilerParams(
            collective_id=0, has_side_effects=True, vmem_limit_bytes=54 * 2**20
        ),
        cost_estimate=pl.CostEstimate(flops=2_000_000_000, bytes_accessed=20_000_000, transcendentals=0),
        name="gather",
    )(w_q, q_latent, latent_bias, steer, d_out, kv_latent, key_rope, w_uk, w_uv, gain)


CHUNK = 256
TILES = CHUNK // BLK


def attend_kernel(
    mask, qg_ref, qr_ref, KV, gl, gr, keys_all, qg, qr, sbuf, dbuf, acc, peak, lsum, gsum, index, sem
):
    c, k, a, z = place()
    scale = HEADW ** (-0.5)
    scale2 = scale * math.log2(math.e)
    rows = HALF * BLK
    loads = [
        pltpu.make_async_copy(qg_ref.at[0], qg.at[0], sem.at[0]),
        pltpu.make_async_copy(qr_ref, qr, sem.at[1]),
        pltpu.make_async_copy(KV, keys_all, sem.at[2]),
        pltpu.make_async_copy(qg_ref.at[1], qg.at[1], sem.at[3]),
    ]
    for copy in loads:
        copy.start()

    live = []
    for i in range(2):
        block = c if i == 0 else lax.rem(c + NZ, 2 * NZ)

        def visit(j, n):
            far = lax.rem(z - lax.rem(j, NZ) + NZ, NZ)
            slot = jnp.where(far == 0, 0, jnp.where(far <= NZ // 2, 2 * far - 1, 2 * (NZ - far)))
            index[i, n] = (j // NZ) * NZ + slot
            return n + jnp.where(mask[block, j] > 0, 1, 0)

        n = lax.fori_loop(0, 2 * NZ, visit, 0)
        for extra in range(TILES - 1):
            index[i, n + extra] = 0
        live.append(n)

    def chunks_of(n):
        return (n + TILES - 1) // TILES

    def keys_of(i, t):
        return jnp.concatenate([keys_all[index[i, t * TILES + d]] for d in range(TILES)], axis=0)

    def in_fours(count, step):
        def four(t, _):
            step(4 * t, 4)
            return 0

        lax.fori_loop(0, count // 4, four, 0)
        rest = lax.rem(count, 4)

        @pl.when(rest >= 2)
        def _():
            step(count - rest, 2)

        @pl.when(lax.rem(rest, 2) == 1)
        def _():
            step(count - 1, 1)

    for i in range(2):
        n = live[i]
        count = chunks_of(n)

        for copy in loads[3 * i : 3 * i + 3]:
            copy.wait()
        peak[...] = jnp.full((rows, 128), LOWEST, F32)
        lsum[...] = jnp.zeros((rows, 128), F32)
        gsum[...] = jnp.zeros((rows, 128), F32)
        acc[...] = jnp.zeros((rows, WIDE), F32)

        def scores(first, many):
            top = peak[...]
            for t in [first + d for d in range(many)]:
                keys = keys_of(i, t)
                column = lax.broadcasted_iota(jnp.int32, (1, CHUNK), 1) + t * CHUNK
                dead = jnp.where(column < n * BLK, 0.0, LOWEST)
                main = last_last(qg[i], keys[:, :KVL])
                s = main[:rows] + last_last(qr[i], keys[:, KVL:]) + dead
                sbuf[t] = s
                dbuf[t] = main[rows:]
                for part in range(TILES):
                    top = jnp.maximum(top, s[:, part * 128 : (part + 1) * 128])
            peak[...] = top

        in_fours(count, scores)
        top = jnp.max(peak[...], axis=1, keepdims=True) * scale2

        def weigh(first, many):
            low = lsum[...]
            gow = gsum[...]
            for t in [first + d for d in range(many)]:
                e = jnp.exp2(sbuf[t] * scale2 - top)
                sbuf[t] = e
                mixed = e * dbuf[t]
                low = low + sum(e[:, p * 128 : (p + 1) * 128] for p in range(TILES))
                gow = gow + sum(mixed[:, p * 128 : (p + 1) * 128] for p in range(TILES))
            lsum[...] = low
            gsum[...] = gow

        in_fours(count, weigh)
        total = jnp.sum(lsum[...], axis=1, keepdims=True)
        ratio = jnp.sum(gsum[...], axis=1, keepdims=True) / total

        def collect(first, many):
            weight = jnp.concatenate(
                [(sbuf[first + d] * (dbuf[first + d] - ratio)).astype(BF16) for d in range(many)], axis=1
            )
            keys = jnp.concatenate([keys_of(i, first + d) for d in range(many)], axis=0)
            acc[...] += jnp.dot(weight, keys, preferred_element_type=F32)

        in_fours(count, collect)
        grad = acc[...] * (scale / total)
        gl[i] = grad[:, :KVL].astype(BF16).reshape(HALF, BLK, KVL)
        gr[i] = grad[:, KVL:].reshape(HALF, BLK, WIDE - KVL)


def attend(mask, qg, qr, KV):
    rows = HALF * BLK
    nchunk = 2 * NZ // TILES
    return pl.pallas_call(
        attend_kernel,
        out_shape=(
            jax.ShapeDtypeStruct((2, HALF, BLK, KVL), BF16),
            jax.ShapeDtypeStruct((2, HALF, BLK, WIDE - KVL), F32),
        ),
        in_specs=[pl.BlockSpec(memory_space=pltpu.SMEM), HBM, HBM, HBM],
        out_specs=[VM, VM],
        scratch_shapes=[
            pltpu.VMEM((2 * NZ, BLK, WIDE), BF16),
            pltpu.VMEM((2, 2 * rows, KVL), BF16),
            pltpu.VMEM((2, rows, WIDE - KVL), BF16),
            pltpu.VMEM((nchunk, rows, CHUNK), F32),
            pltpu.VMEM((nchunk, rows, CHUNK), F32),
            pltpu.VMEM((rows, WIDE), F32),
            pltpu.VMEM((rows, 128), F32),
            pltpu.VMEM((rows, 128), F32),
            pltpu.VMEM((rows, 128), F32),
            pltpu.SMEM((2, 2 * NZ + TILES), jnp.int32),
            pltpu.SemaphoreType.DMA((4,)),
        ],
        compiler_params=pltpu.CompilerParams(vmem_limit_bytes=54 * 2**20),
        cost_estimate=pl.CostEstimate(flops=10_000_000_000, bytes_accessed=10_000_000, transcendentals=4_000_000),
        name="attend",
    )(mask, qg, qr, KV)


def reduce_kernel(
    q_ref, xq_ref, b_ref, xb_ref, gain_ref, W_ref, uk_ref, pj_ref, gl_ref, gr_ref,
    steer_out, bias_out,
    q2, Wv, uk, pj, gl, gr, u_ref, gs_ref, lb_ref, rbuf, rgs, p_s, p_r, g_s, g_r, sem,
):
    c, k, a, z = place()
    pair_c = (1 - a) * NZ + z
    n = 16

    def mate(side, shift):
        return (pair_c if side else c, lax.rem(k + shift, n))

    my_d = pl.ds(pl.multiple_of(a * DCOLS, 128), DCOLS)
    loads = [
        pltpu.make_async_copy(gl_ref, gl, sem.at[0]),
        pltpu.make_async_copy(uk_ref.at[:, my_d], uk, sem.at[1]),
        pltpu.make_async_copy(gr_ref, gr, sem.at[2]),
        pltpu.make_async_copy(pj_ref, pj, sem.at[3]),
        pltpu.make_async_copy(q_ref, q2.at[0], sem.at[4]),
        pltpu.make_async_copy(xq_ref, q2.at[1], sem.at[5]),
        pltpu.make_async_copy(W_ref, Wv, sem.at[6]),
    ]
    for load in loads:
        load.start()
    others = [(side, shift) for side in range(2) for shift in range(n) if side or shift]
    barrier = pltpu.get_barrier_semaphore()
    for one in others:
        pl.semaphore_signal(barrier, inc=1, device_id=mate(*one), device_id_type=MESH)
    both = 2 * BLK
    gain = gain_ref[...].reshape(1, gain_ref.shape[0])
    for load in loads:
        load.wait()
    pieces = []
    for h in range(HALF):
        pieces.append(
            jnp.dot(gl[:, h].reshape(both, KVL), uk[:, h * NOPE : (h + 1) * NOPE], preferred_element_type=F32)
        )
        pieces.append(gr[:, h].reshape(both, WIDE - KVL)[:, :ROPE])
    all_grads = jnp.concatenate(pieces, axis=1)
    u_ref[...] = jnp.zeros_like(u_ref)
    for i in range(2):
        shifted = q2[i].astype(F32) + (b_ref, xb_ref)[i][...]
        inv = lax.rsqrt(jnp.mean(shifted * shifted, axis=1, keepdims=True) + EPS)
        grad_query = all_grads[i * BLK : (i + 1) * BLK]
        gs_ref[i : i + 1, :] = jnp.sum(grad_query, axis=0, keepdims=True)
        lean = sum(
            jnp.sum(
                grad_query[:, two * QTWO : (two + 1) * QTWO] * pj[two, i * BLK : (i + 1) * BLK, :], axis=1, keepdims=True
            )
            for two in range(2)
        )
        u = jnp.sum(grad_query * inv, axis=0, keepdims=True)
        u_high = u.astype(BF16)
        u_ref[2 * i : 2 * i + 1, :] = u_high.astype(F32)
        u_ref[2 * i + 1 : 2 * i + 2, :] = u - u_high.astype(F32)
        lb_ref[i : i + 1, :] = jnp.sum(shifted * (inv * inv * lean), axis=0, keepdims=True)

    back = sum(
        last_last(u_ref[:, two * QTWO : (two + 1) * QTWO].astype(BF16), Wv[two]) for two in range(2)
    )
    for i in range(2):
        whole = back[2 * i : 2 * i + 1] + back[2 * i + 1 : 2 * i + 2]
        lb_ref[i : i + 1, :] = gain * whole - lb_ref[i : i + 1, :] * (1.0 / gain.shape[1])
    pl.semaphore_wait(barrier, len(others))

    def copy(src, dst, s, r, dev):
        return pltpu.make_async_remote_copy(
            src_ref=src, dst_ref=dst, send_sem=s, recv_sem=r, device_id=dev, device_id_type=MESH
        )

    steer_copy = copy(gs_ref.at[pl.ds(1, 1)], rgs, p_s.at[0], p_r.at[0], mate(1, 0))
    steer_copy.start()
    out = []
    for side, shift in others:
        at = side * n + shift
        out.append(
            copy(lb_ref.at[pl.ds(side, 1)], rbuf.at[at], g_s.at[at], g_r.at[at], mate(side, shift))
        )
        out[-1].start()
    steer_copy.wait_recv()
    mine = gs_ref[0:1, :]
    theirs = rgs[...]
    steer_out[:, :QCOLS] = jnp.where(a == 0, mine, theirs)
    steer_out[:, QCOLS:] = jnp.where(a == 0, theirs, mine)
    result = lb_ref[0:1, :]
    for (side, shift), one in zip(others, out):
        one.wait_recv()
        result = result + rbuf[side * n + shift]
    bias_out[...] = result
    steer_copy.wait_send()
    for one in out:
        one.wait_send()


def reduce(q, xq, b, xb, gain, W, w_uk, pj, gl, gr):
    ql = q.shape[1]
    return pl.pallas_call(
        reduce_kernel,
        out_shape=(jax.ShapeDtypeStruct((1, 2 * QCOLS), F32), jax.ShapeDtypeStruct((1, ql), F32)),
        in_specs=[HBM, HBM, VM, VM, VM, HBM, HBM, HBM, HBM, HBM],
        out_specs=[VM, VM],
        scratch_shapes=[
            pltpu.VMEM((2, BLK, ql), BF16),
            pltpu.VMEM((2, ql, QTWO), BF16),
            pltpu.VMEM((KVL, DCOLS), BF16),
            pltpu.VMEM((2, 2 * BLK, QTWO), F32),
            pltpu.VMEM((2, HALF, BLK, KVL), BF16),
            pltpu.VMEM((2, HALF, BLK, WIDE - KVL), F32),
            pltpu.VMEM((16, QCOLS), F32),
            pltpu.VMEM((2, QCOLS), F32),
            pltpu.VMEM((2, ql), F32),
            pltpu.VMEM((32, 1, ql), F32),
            pltpu.VMEM((1, QCOLS), F32),
            pltpu.SemaphoreType.DMA((1,)),
            pltpu.SemaphoreType.DMA((1,)),
            pltpu.SemaphoreType.DMA((32,)),
            pltpu.SemaphoreType.DMA((32,)),
            pltpu.SemaphoreType.DMA((7,)),
        ],
        compiler_params=pltpu.CompilerParams(
            collective_id=1, has_side_effects=True, vmem_limit_bytes=54 * 2**20
        ),
        name="reduce",
    )(q, xq, b, xb, gain, W, w_uk, pj, gl, gr)


def shards(
    q_latent, latent_bias, norm_gain, w_q, steer, kv_latent, key_rope, w_uk, w_uv, d_out, block_mask
):
    ql = q_latent.shape[1]
    W, KV, xq, xb, qg, qr, pj = gather(
        w_q, q_latent, latent_bias, steer, d_out, kv_latent, key_rope.T, w_uk, w_uv, norm_gain
    )
    gl, gr = attend(block_mask, qg, qr, KV.reshape(2 * NZ, BLK, WIDE))
    grad_steer, grad_bias = reduce(
        q_latent, xq, latent_bias, xb, norm_gain, W.reshape(2, ql, QTWO), w_uk, pj, gl, gr
    )
    return (grad_steer, grad_bias)


def solution(mesh):
    in_specs = (
        P("ctx", None),
        P("ctx", None),
        P(),
        P("ctx", "head"),
        P("ctx", "head"),
        P("ctx", None),
        P("ctx", None),
        P(None, "head"),
        P(None, "head"),
        P("ctx", "head"),
        P(),
    )
    out_specs = (P("ctx", "head"), P("ctx", None))
    return jax.shard_map(shards, mesh=mesh, in_specs=in_specs, out_specs=out_specs, check_vma=False)
```
